128 devices in a mesh: dp: 32 (over x, z, y_lo), tensor: 4 (over y_hi, core).
Axes of the slice: x: 4, y: 4 (y_hi: 2, y_lo: 2; y = y_hi * 2 + y_lo), z: 4, core: 2. Of those that a mesh axis runs over, the one named last changes fastest.
Arguments:
- tokens: bfloat16 [32768, 1024], P(('dp', 'tensor')), may hold values from -24 to 24
- cotangent: bfloat16 [32768, 1024], P(('dp', 'tensor')), may hold values from -24 to 24
- segments: int32 [32768], P('dp'), may hold values from 0 to 3, as said below
- ln1_gain: bfloat16 [1024], P('dp'), may hold values from 0.5 to 1.5
- ln1_bias: bfloat16 [1024], P('dp'), may hold values from -1.25 to 1.25
- w_qkv: bfloat16 [1024, 3, 1024], P('dp', None, 'tensor'), may hold values from -0.1875 to 0.1875
- bias_qv: bfloat16 [2, 16, 64], P(None, 'tensor', 'dp'), may hold values from -1.75 to 1.75
- w_out: bfloat16 [1024, 1024], P('tensor', 'dp'), may hold values from -0.375 to 0.375
- bias_out: bfloat16 [1024], P('dp'), may hold values from -1.25 to 1.25
- ln2_gain: bfloat16 [1024], P('dp'), may hold values from 0.5 to 1.5
- ln2_bias: bfloat16 [1024], P('dp'), may hold values from -1.25 to 1.25
- w_fc: bfloat16 [1024, 4096], P('dp', 'tensor'), may hold values from -0.1875 to 0.1875
- bias_fc: bfloat16 [32, 128], P('tensor', 'dp'), may hold values from -1.75 to 1.75
- w_proj: bfloat16 [4096, 1024], P('tensor', 'dp'), may hold values from -0.09375 to 0.09375
- bias_proj: bfloat16 [1024], P('dp'), may hold values from -1.25 to 1.25
Outputs:
- mixed: bfloat16 [32768, 1024], P(('dp', 'tensor'))
- input_grad: float32 [32768, 1024], P(('dp', 'tensor'))
- grad_ln1_gain: float32 [1024], P(('dp', 'tensor'))
- grad_ln1_bias: float32 [1024], P(('dp', 'tensor'))
- grad_qkv: float32 [1024, 3, 1024], P('dp', None, 'tensor')
- grad_bias_qv: float32 [2, 16, 64], P(None, 'tensor', 'dp')
- grad_out: float32 [1024, 1024], P('tensor', 'dp')
- grad_bias_out: float32 [1024], P('dp')
- grad_ln2_gain: float32 [1024], P(('dp', 'tensor'))
- grad_ln2_bias: float32 [1024], P(('dp', 'tensor'))
- grad_fc: float32 [1024, 4096], P('dp', 'tensor')
- grad_bias_fc: float32 [32, 128], P('tensor', 'dp')
- grad_proj: float32 [4096, 1024], P('tensor', 'dp')
- grad_bias_proj: float32 [1024], P('dp')
The draws below stay inside these ranges and needn't reach their ends.
Inputs may be any that keep to these rules, and one draw needn't show every extreme that they name: `segments`: within each sequence of 1024 tokens the numbers start at 0, never fall and rise by one at three document bounds; the second document begins within the first 128 tokens and ends within the last 128.
All inputs are finite; a program needn't handle non-finite values.
Results may differ from the reference program's by a relative error of at most 0.014.
Values may be sent and summed in bfloat16 or wider, within the bound.
No kernel may reach another device: no remote copies, remote signals or barrier semaphores. Data moves between devices by JAX's collectives and lax.ppermute only.
A program may use at most 128 MiB of HBM per device.

```python
import math
import jax
import jax.numpy as jnp
from jax import lax

D = 1024
HEADS = 16
HD = 64
FF = 4096
SEQ = 1024
TOKENS = 32768


def draw_segments(key, part):
    key = jax.random.fold_in(key, 7)
    first_key, second_key, third_key = jax.random.split(key, 3)
    seq_total = TOKENS // SEQ
    margin = SEQ // 8
    opening = jax.random.randint(first_key, (seq_total, 1), 1, margin)
    closing = jax.random.randint(second_key, (seq_total, 1), SEQ - margin, SEQ - 1)
    spread_draw = jax.random.randint(third_key, (seq_total, 1), 0, SEQ)
    trailing = closing + 1 + spread_draw % (SEQ - 1 - closing)
    places = jnp.arange(SEQ, dtype=jnp.int32)[None, :]
    labels = (places >= opening).astype(jnp.int32) + (places >= closing).astype(jnp.int32) + (places >= trailing).astype(jnp.int32)
    return labels.reshape(TOKENS)


def with_spikes(values, key, source, target, blocks, factor):
    owner, partner = [(jnp.arange(values.shape[axis_at]) // (values.shape[axis_at] // blocks)).reshape([-1 if axis == axis_at else 1 for axis in range(values.ndim)]) for axis_at in (source, target)]
    chosen = jax.random.permutation(key, blocks)[partner]
    strong = (owner == chosen) | (owner == (partner + blocks // 2) % blocks)
    return jnp.where(strong, factor * values, values)


def level_of(own_key, dims, shards, low, largest):
    def one(axis_at, shards_of):
        draws = jax.random.uniform(jax.random.fold_in(jax.random.fold_in(own_key, 6), axis_at), (shards_of,), jnp.float32, low / len(shards), largest / len(shards))
        return jnp.repeat(jnp.exp(draws), dims[axis_at] // shards_of).reshape((-1,) + (1,) * (len(dims) - axis_at - 1))

    gain = one(*shards[0])
    for cut in shards[1:]:
        gain = gain * one(*cut)
    return gain


def noise(rng, shape, scale, reach, shards=(), held_as=jnp.bfloat16):
    loudness = level_of(rng, shape, shards, -0.22, 0.18) if shards else 1.0
    drawn = jax.random.normal(rng, shape, jnp.float32) * scale * loudness
    return jnp.minimum(jnp.maximum(drawn, -reach), reach).astype(held_as)


def heavy_noise(stream_key, extent, spread, limit, cuts, heavy, kind=jnp.bfloat16):
    entries = spread * jax.random.normal(stream_key, extent, jnp.float32)
    if cuts:
        entries = entries * level_of(stream_key, extent, cuts, -0.22, 0.18)
    return jnp.clip(with_spikes(entries, jax.random.fold_in(stream_key, 3), *heavy), -limit, limit).astype(kind)


def setup_inputs(seed: int = 0) -> dict:
    arg_keys = jax.random.split(jax.random.key(seed), 16)
    tokens = heavy_noise(arg_keys[0], (TOKENS, D), 1.0, 24.0, ((0, 128),), (0, 1, 128, 5.5))
    cotangent = heavy_noise(arg_keys[1], (TOKENS, D), 1.0, 24.0, ((0, 128),), (0, 1, 128, 5.5))
    segments = draw_segments(jax.random.fold_in(arg_keys[15], 71), 0)
    ln1_gain = jnp.clip(1.0 + 0.1 * jax.random.normal(arg_keys[3], (D,), jnp.float32), 0.5, 1.5).astype(jnp.bfloat16)
    ln1_bias = noise(arg_keys[4], (D,), 0.2, 1.25, ((0, 32),))
    w_qkv = noise(arg_keys[5], (D, 3, D), D ** -0.5, 0.1875, ((0, 32), (2, 4)))
    bias_qv = noise(arg_keys[6], (2, HEADS, HD), 0.3, 1.75, ((1, 4), (2, 32)))
    w_out = noise(arg_keys[7], (D, D), (D // 4) ** -0.5, 0.375, ((0, 4), (1, 32)))
    bias_out = noise(arg_keys[8], (D,), 0.2, 1.25, ((0, 32),))
    ln2_gain = jnp.clip(1.0 + 0.1 * jax.random.normal(arg_keys[9], (D,), jnp.float32), 0.5, 1.5).astype(jnp.bfloat16)
    ln2_bias = noise(arg_keys[10], (D,), 0.2, 1.25, ((0, 32),))
    w_fc = noise(arg_keys[11], (D, FF), D ** -0.5, 0.1875, ((0, 32), (1, 4)))
    bias_fc = noise(arg_keys[12], (FF // 128, 128), 0.3, 1.75, ((0, 4), (1, 32)))
    w_proj = noise(arg_keys[13], (FF, D), FF ** -0.5, 0.09375, ((0, 4), (1, 32)))
    bias_proj = noise(arg_keys[14], (D,), 0.2, 1.25, ((0, 32),))
    return {"tokens": tokens, "cotangent": cotangent, "segments": segments, "ln1_gain": ln1_gain, "ln1_bias": ln1_bias, "w_qkv": w_qkv, "bias_qv": bias_qv, "w_out": w_out, "bias_out": bias_out, "ln2_gain": ln2_gain, "ln2_bias": ln2_bias, "w_fc": w_fc, "bias_fc": bias_fc, "w_proj": w_proj, "bias_proj": bias_proj}


@jax.custom_vjp
def low(v):
    return lax.optimization_barrier(v.astype(jnp.bfloat16)).astype(jnp.float32)

@jax.custom_vjp
def low_back(v):
    return v

def low_keep(v):
    return (low(v), None)

def low_pass(kept, grad):
    return (grad,)

def back_keep(v):
    return (v, None)

def back_low(kept, grad):
    return (low(grad),)
low.defvjp(low_keep, low_pass)
low_back.defvjp(back_keep, back_low)

def layer_norm(values, scales, offsets):
    centered = values - lax.optimization_barrier(jnp.mean(values, axis=-1, keepdims=True))
    variance = lax.optimization_barrier(jnp.mean(centered * centered, axis=-1, keepdims=True))
    return centered * lax.rsqrt(variance + 1e-05) * scales + offsets

def attend_sequence(queries, key_rows, values, labels):
    block_rows = min(512, SEQ)
    block_count = SEQ // block_rows
    scale_factor = HD ** (-0.5)
    key_places = jnp.arange(SEQ, dtype=jnp.int32)

    @jax.checkpoint
    def one_block(number):
        offset_row = number * block_rows
        query_rows = lax.dynamic_slice_in_dim(queries, offset_row, block_rows, 0)
        label_rows = lax.dynamic_slice_in_dim(labels, offset_row, block_rows, 0)
        row_places = offset_row + jnp.arange(block_rows, dtype=jnp.int32)
        raw_scores = low_back(jnp.einsum('qhd,khd->hqk', query_rows, key_rows, precision=lax.Precision.HIGHEST) * scale_factor)
        allowed = (label_rows[:, None] == labels[None, :]) & (key_places[None, :] <= row_places[:, None])
        scores = jnp.where(allowed[None], raw_scores, -1e+30)
        attention_weights = low(jax.nn.softmax(scores, axis=-1))
        return jnp.einsum('hqk,khd->qhd', attention_weights, values, precision=lax.Precision.HIGHEST)
    blocks = lax.map(one_block, jnp.arange(block_count, dtype=jnp.int32))
    return blocks.reshape(SEQ, HEADS, HD)

def forward(inputs, labels, weights):
    gain_one, shift_one, qkv_weight, qv_bias, out_weight, out_bias, gain_two, shift_two, fc_weight, fc_bias, proj_weight, proj_bias = weights
    highest = lax.Precision.HIGHEST
    normed_one = low(layer_norm(inputs, gain_one, shift_one))
    bias_rows = jnp.stack([qv_bias[0].reshape(D), jnp.zeros((D,), jnp.float32), qv_bias[1].reshape(D)])
    joined_rows = low_back(low(jnp.einsum('gtd,dce->gtce', normed_one, qkv_weight, precision=highest) + bias_rows))
    head_shape = inputs.shape[:2] + (HEADS, HD)
    context = jax.vmap(attend_sequence)(joined_rows[:, :, 0].reshape(head_shape), joined_rows[:, :, 1].reshape(head_shape), joined_rows[:, :, 2].reshape(head_shape), labels)
    context = low_back(low(context.reshape(inputs.shape)))
    branch_attn = low_back(jnp.einsum('gtd,de->gte', context, out_weight, precision=highest) + out_bias)
    middle = inputs + branch_attn
    normed_two = low(layer_norm(middle, gain_two, shift_two))
    hidden = low_back(jnp.einsum('gtd,df->gtf', normed_two, fc_weight, precision=highest) + fc_bias.reshape(FF))
    active = low(jax.nn.gelu(hidden, approximate=True))
    branch_mlp = low_back(jnp.einsum('gtf,fd->gtd', active, proj_weight, precision=highest) + proj_bias)
    return middle + branch_mlp

def reference(tokens, cotangent, segments, ln1_gain, ln1_bias, w_qkv, bias_qv, w_out, bias_out, ln2_gain, ln2_bias, w_fc, bias_fc, w_proj, bias_proj):
    weights = tuple((item.astype(jnp.float32) for item in (ln1_gain, ln1_bias, w_qkv, bias_qv, w_out, bias_out, ln2_gain, ln2_bias, w_fc, bias_fc, w_proj, bias_proj)))
    seq_total = TOKENS // SEQ
    bundle = math.gcd(seq_total, max(1, 4096 // SEQ))
    rounds = seq_total // bundle
    input_view = tokens.astype(jnp.float32).reshape(rounds, bundle, SEQ, D)
    cot_view = cotangent.astype(jnp.float32).reshape(rounds, bundle, SEQ, D)
    label_view = segments.reshape(rounds, bundle, SEQ)

    def advance(totals, pieces):
        input_part, cot_part, label_part = pieces
        result, pull = jax.vjp(lambda inner_in, inner_weights: forward(inner_in, label_part, inner_weights), input_part, weights)
        d_inputs, d_weights = pull(cot_part)
        return (jax.tree.map(jnp.add, totals, d_weights), (result.astype(jnp.bfloat16), d_inputs))
    initial = jax.tree.map(jnp.zeros_like, weights)
    totals, (results, d_inputs) = lax.scan(advance, initial, (input_view, cot_view, label_view))
    return (results.reshape(TOKENS, D), d_inputs.reshape(TOKENS, D), totals[0], totals[1], totals[2], totals[3], totals[4], totals[5], totals[6], totals[7], totals[8], totals[9], totals[10], totals[11])
```

```python
import functools

import jax
import jax.numpy as jnp
from jax import lax
from jax.experimental import pallas as pl
from jax.experimental.pallas import tpu as pltpu
from jax.sharding import Mesh
from jax.sharding import PartitionSpec as P

HD = 64
SEQ = 1024
D = 1024
BLK = 256
HALF = 512
EPS = 1e-05
GELU_C = 0.7978845608028654
GELU_A = 0.044715
DP = ("x", "z", "yl")
TP = ("yh", "core")
ALL = DP + TP
SWAP = [(0, 1), (1, 0)]
f32 = jnp.float32
bf16 = jnp.bfloat16
VMEM_BYTES = 50 * 1024 * 1024


def kernel_call(body, grid, in_specs, out_specs, out_shape, flops, prefetch=0, scratch=()):
    return pl.pallas_call(
        body,
        out_shape=out_shape,
        grid_spec=pltpu.PrefetchScalarGridSpec(
            num_scalar_prefetch=prefetch,
            grid=grid,
            in_specs=in_specs,
            out_specs=out_specs,
            scratch_shapes=scratch,
        ),
        compiler_params=pltpu.CompilerParams(vmem_limit_bytes=VMEM_BYTES),
        cost_estimate=pl.CostEstimate(flops=flops, bytes_accessed=8 << 20, transcendentals=0),
    )


def shape(dims, dtype):
    return jax.ShapeDtypeStruct(dims, dtype)


def mm(a, b):
    return jnp.dot(a, b, preferred_element_type=f32)


def mm_nt(a, b):
    return lax.dot_general(a, b, (((1,), (1,)), ((), ())), preferred_element_type=f32)


def mm_tn(a, b):
    return lax.dot_general(a, b, (((0,), (0,)), ((), ())), preferred_element_type=f32)


def normalized(values):
    centered = values - jnp.mean(values, axis=-1, keepdims=True)
    variance = jnp.mean(centered * centered, axis=-1, keepdims=True)
    root = lax.rsqrt(variance + EPS)
    return centered * root, root


def norm_pull(grad, xhat, root, gain):
    scaled = grad * gain
    return root * (
        scaled
        - jnp.mean(scaled, axis=-1, keepdims=True)
        - xhat * jnp.mean(scaled * xhat, axis=-1, keepdims=True)
    )


def rows(width, move=lambda i: i, height=BLK):
    return pl.BlockSpec((height, width), lambda i, *_: (move(i), 0))


def whole(dims):
    return pl.BlockSpec(dims, lambda *_: (0,) * len(dims))


def qkv_body(x_ref, w_ref, small_ref, bias_ref, n_ref, j_ref):
    xhat, _ = normalized(x_ref[...].astype(f32))
    low = (xhat * small_ref[0:1, :] + small_ref[1:2, :]).astype(bf16)
    n_ref[...] = low
    j_ref[...] = (mm(low, w_ref[:, :768]) + bias_ref[...]).astype(bf16)


def qkv_rows(x_all, packed, smalls, bias_row):
    return kernel_call(
        qkv_body,
        (4,),
        [rows(D), whole((D, 896)), whole((8, D)), whole((1, 768))],
        [rows(D), rows(768)],
        [shape((SEQ, D), bf16), shape((SEQ, 768), bf16)],
        2 * SEQ * D * 768,
    )(x_all, packed, smalls, bias_row)


def allowed_block(segc_ref, segr_ref, s):
    width = (s + 1) * BLK
    same = segc_ref[s * BLK : width, :] == segr_ref[:, :width]
    row_at = lax.broadcasted_iota(jnp.int32, (BLK, width), 0) + s * BLK
    key_at = lax.broadcasted_iota(jnp.int32, (BLK, width), 1)
    return same & (key_at <= row_at)


def place(loc_ref, s):
    return pl.ds(pl.multiple_of(loc_ref[s] * BLK, BLK), BLK)


def softmax_rows(scores, mask):
    scores = jnp.where(mask, scores, -1e30)
    highest = jnp.max(scores, axis=-1, keepdims=True)
    expanded = jnp.exp(scores - highest)
    return expanded * (1.0 / jnp.sum(expanded, axis=-1, keepdims=True))


def attend_body(loc_ref, segc_ref, segr_ref, q_ref, k_ref, v_ref, o_ref, kn, vn):
    first = lax.broadcasted_iota(jnp.int32, (1, 128), 1) < HD
    for s in range(4):
        kn[s * BLK : (s + 1) * BLK, :] = k_ref[place(loc_ref, s), :]
        vn[s * BLK : (s + 1) * BLK, :] = v_ref[place(loc_ref, s), :]
    for s in range(4):
        width = (s + 1) * BLK
        mask = allowed_block(segc_ref, segr_ref, s)
        q = q_ref[place(loc_ref, s), :] * jnp.asarray(HD**-0.5, bf16)
        done = []
        for mine in (first, ~first):
            qh = jnp.where(mine, q, jnp.zeros_like(q))
            probs = softmax_rows(mm_nt(qh, kn[:width, :]), mask).astype(bf16)
            done.append(mm(probs, vn[:width, :]))
        o_ref[place(loc_ref, s), :] = jnp.where(first, done[0], done[1]).astype(bf16)


def column_block(at):
    return pl.BlockSpec((SEQ, 128), lambda p, *_: (0, at + p))


def attend_forward(loc, segc, segr, joined):
    return kernel_call(
        attend_body,
        (2,),
        [whole((SEQ, 1)), whole((1, SEQ)), column_block(0), column_block(2), column_block(4)],
        column_block(0),
        shape((SEQ, 256), bf16),
        4 * SEQ * SEQ * 256,
        prefetch=1,
        scratch=[pltpu.VMEM((SEQ, 128), bf16)] * 2,
    )(loc, segc, segr, joined, joined, joined)


def attend_back_body(
    loc_ref, segc_ref, segr_ref, q_ref, k_ref, v_ref, d_ref, dq_ref, dk_ref, dv_ref, kn, vn, dk, dv
):
    first = lax.broadcasted_iota(jnp.int32, (1, 128), 1) < HD
    for s in range(4):
        kn[s * BLK : (s + 1) * BLK, :] = k_ref[place(loc_ref, s), :]
        vn[s * BLK : (s + 1) * BLK, :] = v_ref[place(loc_ref, s), :]
    for s in (3, 2, 1, 0):
        width = (s + 1) * BLK
        mask = allowed_block(segc_ref, segr_ref, s)
        q = q_ref[place(loc_ref, s), :] * jnp.asarray(HD**-0.5, bf16)
        d = d_ref[place(loc_ref, s), :]
        keys = kn[:width, :]
        values = vn[:width, :]
        dq_sum, dk_sum, dv_sum = [], [], []
        for mine in (first, ~first):
            qh = jnp.where(mine, q, jnp.zeros_like(q))
            dh = jnp.where(mine, d, jnp.zeros_like(d))
            probs = softmax_rows(mm_nt(qh, keys), mask)
            d_probs = mm_nt(dh, values)
            d_scores = (
                probs * (d_probs - jnp.sum(probs * d_probs, axis=-1, keepdims=True))
            ).astype(bf16)
            dq_sum.append(mm(d_scores, keys))
            dk_sum.append(mm_tn(d_scores, qh))
            dv_sum.append(mm_tn(probs.astype(bf16), dh))
        dq = jnp.where(first, dq_sum[0], dq_sum[1]) * (HD**-0.5)
        dq_ref[place(loc_ref, s), :] = dq.astype(bf16)
        if s == 3:
            dk[...] = dk_sum[0] + dk_sum[1]
            dv[...] = dv_sum[0] + dv_sum[1]
        else:
            dk[:width, :] += dk_sum[0] + dk_sum[1]
            dv[:width, :] += dv_sum[0] + dv_sum[1]
    for s in range(4):
        dk_ref[place(loc_ref, s), :] = dk[s * BLK : (s + 1) * BLK, :].astype(bf16)
        dv_ref[place(loc_ref, s), :] = dv[s * BLK : (s + 1) * BLK, :].astype(bf16)


def attend_backward(loc, segc, segr, joined, d_context):
    return kernel_call(
        attend_back_body,
        (2,),
        [
            whole((SEQ, 1)),
            whole((1, SEQ)),
            column_block(0),
            column_block(2),
            column_block(4),
            column_block(0),
        ],
        [column_block(0)] * 3,
        [shape((SEQ, 256), bf16)] * 3,
        10 * SEQ * SEQ * 256,
        prefetch=1,
        scratch=[pltpu.VMEM((SEQ, 128), bf16)] * 2 + [pltpu.VMEM((SEQ, 128), f32)] * 2,
    )(loc, segc, segr, joined, joined, joined, d_context)


def out_other_body(c_ref, w_ref, o_ref):
    o_ref[...] = mm_nt(c_ref[...], w_ref[...]).astype(bf16)


OUT_COLUMNS = pl.BlockSpec((D, 256), lambda *_: (0, 8))
FC_COLUMNS = pl.BlockSpec((D, D), lambda *_: (0, 0))
PROJ_COLUMNS = pl.BlockSpec((D, D), lambda *_: (0, 1))


def out_other(context, packed):
    return kernel_call(
        out_other_body,
        (2,),
        [rows(256, lambda i: i + 2), OUT_COLUMNS],
        rows(D),
        shape((HALF, D), bf16),
        2 * HALF * D * 256,
    )(context, packed)


def out_mine_body(c_ref, w_ref, r_ref, s_ref, low_ref):
    total = mm_nt(c_ref[...], w_ref[...]) + r_ref[...].astype(f32)
    s_ref[...] = total
    low_ref[...] = total.astype(bf16)


def out_mine(context, packed, received):
    return kernel_call(
        out_mine_body,
        (2,),
        [rows(256), OUT_COLUMNS, rows(D)],
        [rows(D), rows(D)],
        [shape((HALF, D), f32), shape((HALF, D), bf16)],
        2 * HALF * D * 256,
    )(context, packed, received)


def middle_body(x_ref, s_ref, r_ref, small_ref, mid_ref, n_ref):
    middle = (
        x_ref[...].astype(f32) + (s_ref[...] + r_ref[...].astype(f32)) + small_ref[2:3, :]
    )
    mid_ref[...] = middle
    xhat, _ = normalized(middle)
    n_ref[...] = (xhat * small_ref[3:4, :] + small_ref[4:5, :]).astype(bf16)


def middle_rows(x_mine, s, r, smalls):
    return kernel_call(
        middle_body,
        (2,),
        [rows(D), rows(D), rows(D, lambda i: 1 - i), whole((8, D))],
        [rows(D), rows(D)],
        [shape((HALF, D), f32), shape((HALF, D), bf16)],
        HALF * D * 10,
    )(x_mine, s, r, smalls)


def feed_body(n_ref, g_ref, fc_ref, proj_ref, b_ref, a_ref, dh_ref, m_ref, dn_ref, sum_ref):
    hidden = mm(n_ref[...], fc_ref[...]) + b_ref[...]
    squared = hidden * hidden
    bent = jnp.tanh(GELU_C * (hidden + GELU_A * (squared * hidden)))
    half = 0.5 * (1.0 + bent)
    active = (hidden * half).astype(bf16)
    slope = half + (0.5 * hidden) * (1.0 - bent * bent) * (
        GELU_C + (3.0 * GELU_A * GELU_C) * squared
    )
    g = g_ref[...]
    d_hidden = (mm(g, proj_ref[...]) * slope).astype(bf16)
    a_ref[...] = active
    dh_ref[...] = d_hidden
    dn_ref[...] = mm_nt(d_hidden, fc_ref[...]).astype(dn_ref.dtype)
    m_ref[...] = mm_nt(active, proj_ref[...]).astype(m_ref.dtype)

    @pl.when(pl.program_id(0) == 0)
    def _():
        sum_ref[...] = jnp.zeros_like(sum_ref)

    sum_ref[0:1, :] += jnp.sum(d_hidden.astype(f32), axis=0, keepdims=True)


def feed_rows(normed, cot, packed, fc_bias, dtype):
    return kernel_call(
        feed_body,
        (2,),
        [rows(D), rows(D), FC_COLUMNS, PROJ_COLUMNS, whole((1, D))],
        [rows(D), rows(D), rows(D), rows(D), whole((8, D))],
        [
            shape((HALF, D), bf16),
            shape((HALF, D), bf16),
            shape((HALF, D), dtype),
            shape((HALF, D), dtype),
            shape((8, D), f32),
        ],
        8 * HALF * D * D,
    )(normed, cot, packed, packed, fc_bias)


def grad_pair_body(a0_ref, a1_ref, b0_ref, b1_ref, o_ref):
    total = mm_tn(a0_ref[...], b0_ref[...]) + mm_tn(a1_ref[...], b1_ref[...])
    o_ref[...] = total.astype(bf16)


def grad_pair(a0, a1, b0, b1):
    width = b0.shape[1]
    return kernel_call(
        grad_pair_body,
        (4,),
        [pl.BlockSpec((HALF, BLK), lambda i: (0, i))] * 2 + [whole((HALF, width))] * 2,
        rows(width),
        shape((D, width), bf16),
        2 * SEQ * D * width,
    )(a0, a1, b0, b1)


def mid_grad_body(s_ref, r_ref, mid_ref, g_ref, small_ref, dm_ref, low_ref, sum_ref):
    d_normed = s_ref[...] + r_ref[...].astype(f32)
    xhat, root = normalized(mid_ref[...])
    g = g_ref[...].astype(f32)
    d_middle = g + norm_pull(d_normed, xhat, root, small_ref[3:4, :])
    dm_ref[...] = d_middle
    low = d_middle.astype(bf16)
    low_ref[...] = low

    @pl.when(pl.program_id(0) == 0)
    def _():
        sum_ref[0:1, :] = jnp.sum(d_normed * xhat, axis=0, keepdims=True)
        sum_ref[1:2, :] = jnp.sum(d_normed, axis=0, keepdims=True)
        sum_ref[2:3, :] = jnp.sum(g, axis=0, keepdims=True)
        sum_ref[3:4, :] = jnp.sum(low.astype(f32), axis=0, keepdims=True)
        sum_ref[4:8, :] = jnp.zeros((4, D), f32)


def mid_grad(s, r, middle, cot_mine, smalls):
    return kernel_call(
        mid_grad_body,
        (2,),
        [rows(D), rows(D, lambda i: 1 - i), rows(D), rows(D), whole((8, D))],
        [rows(D), rows(D), whole((8, D))],
        [shape((HALF, D), f32), shape((HALF, D), bf16), shape((8, D), f32)],
        HALF * D * 20,
    )(s, r, middle, cot_mine, smalls)


def context_grad_body(d0_ref, d1_ref, w_ref, o_ref):
    o_ref[:HALF, :] = mm(d0_ref[...], w_ref[...]).astype(bf16)
    o_ref[HALF:, :] = mm(d1_ref[...], w_ref[...]).astype(bf16)


def context_grad(d0, d1, packed):
    return kernel_call(
        context_grad_body,
        (1,),
        [whole((HALF, D))] * 2 + [OUT_COLUMNS],
        whole((SEQ, 256)),
        shape((SEQ, 256), bf16),
        2 * SEQ * D * 256,
    )(d0, d1, packed)


def norm_one_body(x_ref, q_ref, k_ref, v_ref, w_ref, o_ref, sum_ref):
    partial = (
        mm_nt(q_ref[...], w_ref[:, :256])
        + mm_nt(k_ref[...], w_ref[:, 256:512])
        + mm_nt(v_ref[...], w_ref[:, 512:768])
    )
    xhat, _ = normalized(x_ref[...].astype(f32))
    o_ref[...] = partial.astype(bf16)

    @pl.when(pl.program_id(0) == 0)
    def _():
        sum_ref[...] = jnp.zeros_like(sum_ref)

    sum_ref[0:1, :] += jnp.sum(partial * xhat, axis=0, keepdims=True)
    sum_ref[1:2, :] += jnp.sum(partial, axis=0, keepdims=True)
    sum_ref[2:3, :256] += jnp.sum(q_ref[...].astype(f32), axis=0, keepdims=True)
    sum_ref[2:3, 256:512] += jnp.sum(v_ref[...].astype(f32), axis=0, keepdims=True)


def norm_one_rows(x_all, dq, dk, dv, packed):
    return kernel_call(
        norm_one_body,
        (4,),
        [rows(D), rows(256), rows(256), rows(256), whole((D, 896))],
        [rows(D), whole((8, D))],
        [shape((SEQ, D), bf16), shape((8, D), f32)],
        2 * SEQ * D * 768,
    )(x_all, dq, dk, dv, packed)


def qkv_grad_body(n_ref, q_ref, k_ref, v_ref, o_ref):
    n = n_ref[...]
    o_ref[:, :256] = mm_tn(n, q_ref[...]).astype(bf16)
    o_ref[:, 256:512] = mm_tn(n, k_ref[...]).astype(bf16)
    o_ref[:, 512:768] = mm_tn(n, v_ref[...]).astype(bf16)


def qkv_grad(normed, dq, dk, dv):
    return kernel_call(
        qkv_grad_body,
        (4,),
        [pl.BlockSpec((SEQ, BLK), lambda i: (0, i))] + [whole((SEQ, 256))] * 3,
        rows(768),
        shape((D, 768), bf16),
        2 * SEQ * D * 768,
    )(normed, dq, dk, dv)


def input_grad_body(x_ref, a_ref, b_ref, c_ref, d_ref, dm_ref, small_ref, o_ref):
    d_normed = (a_ref[...].astype(f32) + b_ref[...].astype(f32)) + (
        c_ref[...].astype(f32) + d_ref[...].astype(f32)
    )
    xhat, root = normalized(x_ref[...].astype(f32))
    o_ref[...] = dm_ref[...] + norm_pull(d_normed, xhat, root, small_ref[0:1, :])


def swap(values, axis):
    return lax.ppermute(values, axis, SWAP)


def to_owners(grad):
    parts = lax.all_to_all(grad.reshape(32, 32, grad.shape[1]), DP, 0, 0, tiled=True)
    return jnp.sum(parts.astype(f32), axis=0)


def shards(
    tokens,
    cotangent,
    segments,
    ln1_gain,
    ln1_bias,
    w_qkv,
    bias_qv,
    w_out,
    bias_out,
    ln2_gain,
    ln2_bias,
    w_fc,
    bias_fc,
    w_proj,
    bias_proj,
):
    yh, core, yl = lax.axis_index("yh"), lax.axis_index("core"), lax.axis_index("yl")
    tiny = jnp.stack(
        [
            ln1_gain,
            ln1_bias,
            bias_out,
            ln2_gain,
            ln2_bias,
            bias_proj,
            jnp.pad(bias_qv.reshape(16), (0, 16)),
            bias_fc.reshape(32),
        ],
        axis=1,
    )
    first_pack = jnp.concatenate(
        [w_qkv.reshape(32, 768), jnp.pad(tiny, ((0, 0), (0, 120)))], axis=1
    )
    packed_qkv = lax.all_to_all(
        jnp.broadcast_to(first_pack, (32, 32, 896)), DP, 0, 0, tiled=True
    ).reshape(D, 896)
    second_pack = jnp.concatenate([w_fc, w_proj.T, w_out.T], axis=1)
    neighbour = swap(second_pack, "yl")
    both = jnp.where(
        yl == 0,
        jnp.concatenate([second_pack, neighbour]),
        jnp.concatenate([neighbour, second_pack]),
    )
    packed = lax.all_gather(both, ("x", "z"), axis=0, tiled=True)

    x_mine = jnp.concatenate([tokens, swap(tokens, "yh")])
    x_all = jnp.concatenate([x_mine, swap(x_mine, "core")])
    cot_mine = jnp.concatenate([cotangent, swap(cotangent, "yh")])
    cot_other = swap(cot_mine, "core")

    small_t = packed_qkv[:, 768:776].T
    smalls = small_t.astype(f32)
    qv = small_t[6].reshape(32, 32)[:, :16].reshape(32, 2, 4, 2).transpose(1, 2, 0, 3)
    qv = qv.reshape(2, 256).astype(f32)
    bias_row = jnp.concatenate([qv[0], jnp.zeros((256,), f32), qv[1]])[None]
    fc_bias = small_t[7].reshape(32, 8, 4).transpose(1, 0, 2).reshape(1, D).astype(f32)

    at = jnp.arange(4, dtype=jnp.int32)
    loc = (at // 2 != yh).astype(jnp.int32) + 2 * (at % 2 != core).astype(jnp.int32)
    segc, segr = segments.reshape(SEQ, 1), segments.reshape(1, SEQ)

    normed_one, joined = qkv_rows(x_all, packed_qkv, smalls, bias_row)
    context = attend_forward(loc, segc, segr, joined)
    received = swap(out_other(context, packed), "core")
    s_out, s_out_low = out_mine(context, packed, received)
    middle, n2_mine = middle_rows(x_mine, s_out, swap(s_out_low, "yh"), smalls)
    n2_other = swap(n2_mine, "core")

    act0, dh0, mlp0, dn0, sum0 = feed_rows(n2_mine, cot_mine, packed, fc_bias, f32)
    act1, dh1, mlp1, dn1, sum1 = feed_rows(n2_other, cot_other, packed, fc_bias, bf16)
    s_dn = dn0 + swap(dn1, "core").astype(f32)
    r_dn = swap(s_dn.astype(bf16), "yh")
    s_mlp = mlp0 + swap(mlp1, "core").astype(f32)
    r_mlp = swap(s_mlp[BLK:].astype(bf16), "yh")
    mixed = (
        middle[:BLK] + (s_mlp[:BLK] + r_mlp.astype(f32)) + smalls[5:6]
    ).astype(bf16)
    grad_fc = to_owners(grad_pair(n2_mine, n2_other, dh0, dh1))
    grad_proj = to_owners(grad_pair(cot_mine, cot_other, act0, act1)).T

    d_middle, d_mid0, mid_sums = mid_grad(s_dn, r_dn, middle, cot_mine, smalls)
    d_mid1 = swap(d_mid0, "core")
    d_context = context_grad(d_mid0, d_mid1, packed)
    grad_out = to_owners(grad_pair(d_mid0, d_mid1, context[:HALF], context[HALF:])).T

    dq, dk, dv = attend_backward(loc, segc, segr, joined, d_context)
    grad_qkv = to_owners(qkv_grad(normed_one, dq, dk, dv)).reshape(32, 3, 256)
    d_n1, one_sums = norm_one_rows(x_all, dq, dk, dv, packed_qkv)
    from_core = swap(d_n1[HALF:], "core")
    s_n1 = d_n1[BLK:HALF].astype(f32) + from_core[BLK:].astype(f32)
    from_far = swap(s_n1.astype(bf16), "yh")
    input_grad = kernel_call(
        input_grad_body,
        (1,),
        [whole((BLK, D))] * 2
        + [whole((BLK, D))] * 4
        + [whole((8, D))],
        whole((BLK, D)),
        shape((BLK, D), f32),
        BLK * D * 20,
    )(
        tokens,
        d_n1[:BLK],
        from_core[:BLK],
        from_far,
        jnp.zeros_like(from_far),
        d_middle[:BLK],
        smalls,
    )

    mine = (jnp.arange(4) == 2 * yh + core).astype(f32)[None, :, None]
    norms = jnp.concatenate([one_sums[0:2], mid_sums[0:2]]).reshape(4, 32, 4, 8)
    biases = mid_sums[2:4].reshape(2, 32, 1, 32)
    fc_sum = (sum0[0] + sum1[0]).reshape(8, 32, 4).transpose(1, 0, 2).reshape(32, 1, 32)
    qv_sum = one_sums[2, :512].reshape(2, 4, 32, 2).transpose(2, 0, 1, 3).reshape(32, 1, 16)
    small_out = jnp.concatenate(
        [norms[0], norms[1], norms[2], norms[3]]
        + [jnp.broadcast_to(biases[k], (32, 4, 32)) for k in range(2)]
        + [fc_sum * mine, qv_sum * mine, jnp.zeros((32, 4, 112), f32)],
        axis=2,
    ).reshape(128, 1, 256)
    small_in = jnp.sum(lax.all_to_all(small_out, ALL, 0, 0, tiled=True), axis=(0, 1))
    return (
        mixed,
        input_grad,
        small_in[0:8],
        small_in[8:16],
        grad_qkv,
        small_in[128:144].reshape(2, 4, 2),
        grad_out,
        small_in[64:96],
        small_in[16:24],
        small_in[24:32],
        grad_fc,
        small_in[96:128].reshape(8, 4),
        grad_proj,
        small_in[32:64],
    )


def solution(mesh):
    fine = Mesh(mesh.devices.reshape(4, 4, 2, 2, 2), ALL)
    tok, dp, tp = P(ALL, None), DP, TP
    return jax.shard_map(
        shards,
        mesh=fine,
        in_specs=(
            tok,
            tok,
            P(dp),
            P(dp),
            P(dp),
            P(dp, None, tp),
            P(None, tp, dp),
            P(tp, dp),
            P(dp),
            P(dp),
            P(dp),
            P(dp, tp),
            P(tp, dp),
            P(tp, dp),
            P(dp),
        ),
        out_specs=(
            tok,
            tok,
            P(ALL),
            P(ALL),
            P(dp, None, tp),
            P(None, tp, dp),
            P(tp, dp),
            P(dp),
            P(ALL),
            P(ALL),
            P(dp, tp),
            P(tp, dp),
            P(tp, dp),
            P(dp),
        ),
        check_vma=False,
    )
```

```python
import functools

import jax
import jax.numpy as jnp
from jax import lax
from jax.experimental import pallas as pl
from jax.experimental.pallas import tpu as pltpu
from jax.sharding import Mesh
from jax.sharding import PartitionSpec as P

HD = 64
SEQ = 1024
D = 1024
BLK = 256
HALF = 512
EPS = 1e-05
GELU_C = 0.7978845608028654
GELU_A = 0.044715
DP = ("x", "z", "yl")
TP = ("yh", "core")
XZ = ("x", "z")
ALL = DP + TP
SWAP = [(0, 1), (1, 0)]
f32 = jnp.float32
bf16 = jnp.bfloat16
VMEM_BYTES = 60 * 1024 * 1024


def kernel_call(body, grid, in_specs, out_specs, out_shape, flops, prefetch=0, scratch=()):
    return pl.pallas_call(
        body,
        out_shape=out_shape,
        grid_spec=pltpu.PrefetchScalarGridSpec(
            num_scalar_prefetch=prefetch,
            grid=grid,
            in_specs=in_specs,
            out_specs=out_specs,
            scratch_shapes=scratch,
        ),
        compiler_params=pltpu.CompilerParams(vmem_limit_bytes=VMEM_BYTES),
        cost_estimate=pl.CostEstimate(flops=flops, bytes_accessed=8 << 20, transcendentals=0),
    )


def shape(dims, dtype):
    return jax.ShapeDtypeStruct(dims, dtype)


def mm(a, b):
    return jnp.dot(a, b, preferred_element_type=f32)


def mm_nt(a, b):
    return lax.dot_general(a, b, (((1,), (1,)), ((), ())), preferred_element_type=f32)


def mm_tn(a, b):
    return lax.dot_general(a, b, (((0,), (0,)), ((), ())), preferred_element_type=f32)


def normalized(values):
    centered = values - jnp.mean(values, axis=-1, keepdims=True)
    variance = jnp.mean(centered * centered, axis=-1, keepdims=True)
    root = lax.rsqrt(variance + EPS)
    return centered * root, root


def norm_pull(grad, xhat, root, gain):
    scaled = grad * gain
    return root * (
        scaled
        - jnp.mean(scaled, axis=-1, keepdims=True)
        - xhat * jnp.mean(scaled * xhat, axis=-1, keepdims=True)
    )


def rows(width, move=lambda i: i, height=BLK):
    return pl.BlockSpec((height, width), lambda i, *_: (move(i), 0))


def whole(dims):
    return pl.BlockSpec(dims, lambda *_: (0,) * len(dims))


def qkv_body(x_ref, w_ref, small_ref, bias_ref, n_ref, j_ref):
    xhat, _ = normalized(x_ref[...].astype(f32))
    low = (xhat * small_ref[0:1, :] + small_ref[1:2, :]).astype(bf16)
    n_ref[...] = xhat.astype(bf16)
    j_ref[...] = (mm(low, w_ref[...]) + bias_ref[...]).astype(bf16)


def qkv_rows(x_all, packed, smalls, bias_row):
    return kernel_call(
        qkv_body,
        (4,),
        [rows(D), whole((D, 768)), whole((8, D)), whole((1, 768))],
        [rows(D), rows(768)],
        [shape((SEQ, D), bf16), shape((SEQ, 768), bf16)],
        2 * SEQ * D * 768,
    )(x_all, packed, smalls, bias_row)


def allowed_block(segc_ref, segr_ref, s):
    width = (s + 1) * BLK
    same = segc_ref[s * BLK : width, :] == segr_ref[:, :width]
    row_at = lax.broadcasted_iota(jnp.int32, (BLK, width), 0) + s * BLK
    key_at = lax.broadcasted_iota(jnp.int32, (BLK, width), 1)
    return same & (key_at <= row_at)


def place(loc_ref, s):
    return pl.ds(pl.multiple_of(loc_ref[s] * BLK, BLK), BLK)


def softmax_rows(scores, mask):
    scores = jnp.where(mask, scores, -1e30)
    highest = jnp.max(scores, axis=-1, keepdims=True)
    expanded = jnp.exp(scores - highest)
    return expanded * (1.0 / jnp.sum(expanded, axis=-1, keepdims=True))


def attend_body(loc_ref, segc_ref, segr_ref, q_ref, k_ref, v_ref, o_ref, kn, vn):
    first = lax.broadcasted_iota(jnp.int32, (1, 128), 1) < HD
    for s in range(4):
        kn[s * BLK : (s + 1) * BLK, :] = k_ref[place(loc_ref, s), :]
        vn[s * BLK : (s + 1) * BLK, :] = v_ref[place(loc_ref, s), :]
    for s in range(4):
        width = (s + 1) * BLK
        mask = allowed_block(segc_ref, segr_ref, s)
        q = q_ref[place(loc_ref, s), :] * jnp.asarray(HD**-0.5, bf16)
        done = []
        for mine in (first, ~first):
            qh = jnp.where(mine, q, jnp.zeros_like(q))
            probs = softmax_rows(mm_nt(qh, kn[:width, :]), mask).astype(bf16)
            done.append(mm(probs, vn[:width, :]))
        o_ref[place(loc_ref, s), :] = jnp.where(first, done[0], done[1]).astype(bf16)


def column_block(at):
    return pl.BlockSpec((SEQ, 128), lambda p, *_: (0, at + p))


def attend_forward(loc, segc, segr, joined):
    return kernel_call(
        attend_body,
        (2,),
        [whole((SEQ, 1)), whole((1, SEQ)), column_block(0), column_block(2), column_block(4)],
        column_block(0),
        shape((SEQ, 256), bf16),
        4 * SEQ * SEQ * 256,
        prefetch=1,
        scratch=[pltpu.VMEM((SEQ, 128), bf16)] * 2,
    )(loc, segc, segr, joined, joined, joined)


def attend_back_body(
    loc_ref, segc_ref, segr_ref, q_ref, k_ref, v_ref, d_ref, dq_ref, dk_ref, dv_ref, kn, vn, dk, dv
):
    first = lax.broadcasted_iota(jnp.int32, (1, 128), 1) < HD
    for s in range(4):
        kn[s * BLK : (s + 1) * BLK, :] = k_ref[place(loc_ref, s), :]
        vn[s * BLK : (s + 1) * BLK, :] = v_ref[place(loc_ref, s), :]
    for s in (3, 2, 1, 0):
        width = (s + 1) * BLK
        mask = allowed_block(segc_ref, segr_ref, s)
        q = q_ref[place(loc_ref, s), :] * jnp.asarray(HD**-0.5, bf16)
        d = d_ref[place(loc_ref, s), :]
        keys = kn[:width, :]
        values = vn[:width, :]
        dq_sum, dk_sum, dv_sum = [], [], []
        for mine in (first, ~first):
            qh = jnp.where(mine, q, jnp.zeros_like(q))
            dh = jnp.where(mine, d, jnp.zeros_like(d))
            probs = softmax_rows(mm_nt(qh, keys), mask)
            d_probs = mm_nt(dh, values)
            d_scores = (
                probs * (d_probs - jnp.sum(probs * d_probs, axis=-1, keepdims=True))
            ).astype(bf16)
            dq_sum.append(mm(d_scores, keys))
            dk_sum.append(mm_tn(d_scores, qh))
            dv_sum.append(mm_tn(probs.astype(bf16), dh))
        dq = jnp.where(first, dq_sum[0], dq_sum[1]) * (HD**-0.5)
        dq_ref[place(loc_ref, s), :] = dq.astype(bf16)
        if s == 3:
            dk[...] = dk_sum[0] + dk_sum[1]
            dv[...] = dv_sum[0] + dv_sum[1]
        else:
            dk[:width, :] += dk_sum[0] + dk_sum[1]
            dv[:width, :] += dv_sum[0] + dv_sum[1]
    for s in range(4):
        dk_ref[place(loc_ref, s), :] = dk[s * BLK : (s + 1) * BLK, :].astype(bf16)
        dv_ref[place(loc_ref, s), :] = dv[s * BLK : (s + 1) * BLK, :].astype(bf16)


def attend_backward(loc, segc, segr, joined, d_context):
    return kernel_call(
        attend_back_body,
        (2,),
        [
            whole((SEQ, 1)),
            whole((1, SEQ)),
            column_block(0),
            column_block(2),
            column_block(4),
            column_block(0),
        ],
        [column_block(0)] * 3,
        [shape((SEQ, 256), bf16)] * 3,
        10 * SEQ * SEQ * 256,
        prefetch=1,
        scratch=[pltpu.VMEM((SEQ, 128), bf16)] * 2 + [pltpu.VMEM((SEQ, 128), f32)] * 2,
    )(loc, segc, segr, joined, joined, joined, d_context)


def out_other_body(c_ref, w_ref, o_ref):
    o_ref[...] = mm_nt(c_ref[...], w_ref[...]).astype(bf16)


OUT_COLUMNS = pl.BlockSpec((D, 256), lambda *_: (0, 3))
FC_COLUMNS = pl.BlockSpec((D, D), lambda *_: (0, 0))
PROJ_COLUMNS = pl.BlockSpec((D, D), lambda *_: (0, 1))


def out_other(context, packed):
    return kernel_call(
        out_other_body,
        (2,),
        [rows(256, lambda i: i + 2), OUT_COLUMNS],
        rows(D),
        shape((HALF, D), bf16),
        2 * HALF * D * 256,
    )(context, packed)


def parted(here_ref, there_ref, values):
    @pl.when(pl.program_id(0) == 0)
    def _():
        here_ref[...] = values

    @pl.when(pl.program_id(0) == 1)
    def _():
        there_ref[...] = values


def out_mine_body(c_ref, w_ref, r_ref, s_ref, here_ref, there_ref):
    total = mm_nt(c_ref[...], w_ref[...]) + r_ref[...].astype(f32)
    s_ref[...] = total
    parted(here_ref, there_ref, total.astype(bf16))


def out_mine(context, packed, received):
    return kernel_call(
        out_mine_body,
        (2,),
        [rows(256), OUT_COLUMNS, rows(D)],
        [rows(D)] + [whole((BLK, D))] * 2,
        [shape((HALF, D), f32)] + [shape((BLK, D), bf16)] * 2,
        2 * HALF * D * 256,
    )(context, packed, received)


def arrived(here_ref, there_ref):
    return jnp.where(pl.program_id(0) == 0, here_ref[...], there_ref[...]).astype(f32)


def middle_body(x_ref, s_ref, here_ref, there_ref, small_ref, mid_ref, n_ref):
    total = s_ref[...] + arrived(here_ref, there_ref)
    middle = x_ref[...].astype(f32) + total + small_ref[2:3, :]
    mid_ref[...] = middle
    xhat, _ = normalized(middle)
    n_ref[...] = (xhat * small_ref[3:4, :] + small_ref[4:5, :]).astype(bf16)


def middle_rows(x_mine, s, here, there, smalls):
    return kernel_call(
        middle_body,
        (2,),
        [rows(D), rows(D)] + [whole((BLK, D))] * 2 + [whole((8, D))],
        [rows(D), rows(D)],
        [shape((HALF, D), f32), shape((HALF, D), bf16)],
        HALF * D * 10,
    )(x_mine, s, here, there, smalls)


def feed_core(n_ref, g_ref, fc_ref, proj_ref, b_ref, a_ref, dh_ref, sum_ref):
    @pl.when(pl.program_id(0) == 0)
    def _():
        sum_ref[...] = jnp.zeros_like(sum_ref)

    for at in range(0, D, BLK):
        cut = slice(at, at + BLK)
        hidden = mm(n_ref[...], fc_ref[:, cut]) + b_ref[:, cut]
        d_active = mm(g_ref[...], proj_ref[:, cut])
        squared = hidden * hidden
        bent = jnp.tanh(hidden * (GELU_C + (GELU_A * GELU_C) * squared))
        half = 0.5 + 0.5 * bent
        slope = half + (0.5 * hidden) * (1.0 - bent * bent) * (
            GELU_C + (3.0 * GELU_A * GELU_C) * squared
        )
        d_hidden = (d_active * slope).astype(bf16)
        a_ref[:, cut] = (hidden * half).astype(bf16)
        dh_ref[:, cut] = d_hidden
        sum_ref[0:1, cut] += jnp.sum(d_hidden.astype(f32), axis=0, keepdims=True)


def feed_other_body(
    n_ref, g_ref, fc_ref, proj_ref, b_ref, a_ref, dh_ref, m_ref, dn_ref, sum_ref
):
    feed_core(n_ref, g_ref, fc_ref, proj_ref, b_ref, a_ref, dh_ref, sum_ref)
    dn_ref[...] = mm_nt(dh_ref[...], fc_ref[...]).astype(bf16)
    m_ref[...] = mm_nt(a_ref[...], proj_ref[...]).astype(bf16)


def feed_other(normed, cot, packed, fc_bias):
    return kernel_call(
        feed_other_body,
        (2,),
        [rows(D), rows(D), FC_COLUMNS, PROJ_COLUMNS, whole((1, D))],
        [rows(D)] * 4 + [whole((8, D))],
        [shape((HALF, D), bf16)] * 4 + [shape((8, D), f32)],
        8 * HALF * D * D,
    )(normed, cot, packed, packed, fc_bias)


def feed_mine_body(
    n_ref,
    g_ref,
    fc_ref,
    proj_ref,
    b_ref,
    r_ref,
    a_ref,
    dh_ref,
    m_ref,
    dn_ref,
    here_ref,
    there_ref,
    sum_ref,
):
    feed_core(n_ref, g_ref, fc_ref, proj_ref, b_ref, a_ref, dh_ref, sum_ref)
    total = mm_nt(dh_ref[...], fc_ref[...]) + r_ref[...].astype(f32)
    dn_ref[...] = total
    parted(here_ref, there_ref, total.astype(bf16))
    m_ref[...] = mm_nt(a_ref[...], proj_ref[...])


def feed_mine(normed, cot, packed, fc_bias, dn_in):
    return kernel_call(
        feed_mine_body,
        (2,),
        [rows(D), rows(D), FC_COLUMNS, PROJ_COLUMNS, whole((1, D)), rows(D)],
        [rows(D)] * 4 + [whole((BLK, D))] * 2 + [whole((8, D))],
        [shape((HALF, D), bf16)] * 2
        + [shape((HALF, D), f32)] * 2
        + [shape((BLK, D), bf16)] * 2
        + [shape((8, D), f32)],
        8 * HALF * D * D,
    )(normed, cot, packed, packed, fc_bias, dn_in)


def feed_grads_body(n0_ref, n1_ref, h0_ref, h1_ref, g0_ref, g1_ref, a0_ref, a1_ref, o_ref):
    o_ref[:, :D] = (mm_tn(n0_ref[...], h0_ref[...]) + mm_tn(n1_ref[...], h1_ref[...])).astype(bf16)
    o_ref[:, D:] = (mm_tn(g0_ref[...], a0_ref[...]) + mm_tn(g1_ref[...], a1_ref[...])).astype(bf16)


def feed_grads(n0, n1, h0, h1, g0, g1, a0, a1):
    part = pl.BlockSpec((HALF, BLK), lambda i: (0, i))
    full = whole((HALF, D))
    return kernel_call(
        feed_grads_body,
        (4,),
        [part, part, full, full, part, part, full, full],
        rows(2 * D),
        shape((D, 2 * D), bf16),
        4 * SEQ * D * D,
    )(n0, n1, h0, h1, g0, g1, a0, a1)


def mid_grad_body(
    s_ref, here_ref, there_ref, mid_ref, g_ref, small_ref, dm_ref, low_ref, sum_ref
):
    d_normed = s_ref[...] + arrived(here_ref, there_ref)
    xhat, root = normalized(mid_ref[...])
    g = g_ref[...].astype(f32)
    d_middle = g + norm_pull(d_normed, xhat, root, small_ref[3:4, :])
    dm_ref[...] = d_middle
    low = d_middle.astype(bf16)
    low_ref[...] = low

    @pl.when(pl.program_id(0) == 0)
    def _():
        sum_ref[0:1, :] = jnp.sum(d_normed * xhat, axis=0, keepdims=True)
        sum_ref[1:2, :] = jnp.sum(d_normed, axis=0, keepdims=True)
        sum_ref[2:3, :] = jnp.sum(g, axis=0, keepdims=True)
        sum_ref[3:4, :] = jnp.sum(low.astype(f32), axis=0, keepdims=True)
        sum_ref[4:8, :] = jnp.zeros((4, D), f32)


def mid_grad(s, here, there, middle, cot_mine, smalls):
    return kernel_call(
        mid_grad_body,
        (2,),
        [rows(D)] + [whole((BLK, D))] * 2 + [rows(D), rows(D), whole((8, D))],
        [rows(D), rows(D), whole((8, D))],
        [shape((HALF, D), f32), shape((HALF, D), bf16), shape((8, D), f32)],
        HALF * D * 20,
    )(s, here, there, middle, cot_mine, smalls)


def context_grad_body(d0_ref, d1_ref, w_ref, o_ref):
    o_ref[:HALF, :] = mm(d0_ref[...], w_ref[...]).astype(bf16)
    o_ref[HALF:, :] = mm(d1_ref[...], w_ref[...]).astype(bf16)


def context_grad(d0, d1, packed):
    return kernel_call(
        context_grad_body,
        (1,),
        [whole((HALF, D))] * 2 + [OUT_COLUMNS],
        whole((SEQ, 256)),
        shape((SEQ, 256), bf16),
        2 * SEQ * D * 256,
    )(d0, d1, packed)


def norm_one_body(q_ref, k_ref, v_ref, w_ref, o_ref):
    o_ref[...] = (
        mm_nt(q_ref[...], w_ref[:, :256])
        + mm_nt(k_ref[...], w_ref[:, 256:512])
        + mm_nt(v_ref[...], w_ref[:, 512:768])
    ).astype(bf16)


def norm_one_rows(dq, dk, dv, packed):
    return kernel_call(
        norm_one_body,
        (4,),
        [rows(256), rows(256), rows(256), whole((D, 768))],
        rows(D),
        shape((SEQ, D), bf16),
        2 * SEQ * D * 768,
    )(dq, dk, dv, packed)


def picked(vector, lane):
    at = lax.broadcasted_iota(jnp.int32, (BLK, vector.shape[1]), 1)
    return jnp.sum(jnp.where(at == lane, vector, 0.0), axis=1, keepdims=True)


def attn_grads_body(
    n_ref, q_ref, k_ref, v_ref, m0_ref, m1_ref, c_ref, w_ref, vec_ref, fc_ref, o_ref, sums
):
    step = pl.program_id(0)

    @pl.when(step == 0)
    def _():
        for p, ref in enumerate((q_ref, k_ref, v_ref)):
            sums[0:1, p * 256 : (p + 1) * 256] = jnp.sum(
                ref[...].astype(f32), axis=0, keepdims=True
            )

    n = n_ref[...]
    gain = w_ref[:, 1024:1025].astype(f32)
    offset = w_ref[:, 1025:1026].astype(f32)
    by_gain = jnp.zeros((BLK, 1), f32)
    by_bias = jnp.zeros((BLK, 1), f32)
    for p, ref in enumerate((q_ref, k_ref, v_ref)):
        cut = slice(p * 256, (p + 1) * 256)
        raw = mm_tn(n, ref[...])
        total = sums[0:1, cut]
        weight = w_ref[:, cut].astype(f32)
        by_gain += jnp.sum(weight * raw, axis=1, keepdims=True)
        by_bias += jnp.sum(weight * total, axis=1, keepdims=True)
        o_ref[:, cut] = (raw * gain + offset * total).astype(bf16)
    o_ref[:, 768:1024] = (
        mm_tn(m0_ref[...], c_ref[:HALF, :]) + mm_tn(m1_ref[...], c_ref[HALF:, :])
    ).astype(bf16)
    row = lax.broadcasted_iota(jnp.int32, (BLK, 1), 0)
    owner, inner = step * (BLK // 32) + row // 32, row % 32
    columns = [by_gain, by_bias] + [picked(vec_ref[k : k + 1, :], row) for k in range(4)]
    columns.append(picked(fc_ref[4:5, :], inner // 4 * 128 + owner * 4 + inner % 4))
    lane = inner % 8 // 2 * HD + owner * 2 + inner % 2
    from_q = picked(sums[0:1, 0:256], lane)
    from_v = picked(sums[0:1, 512:768], lane)
    columns.append(jnp.where(inner < 8, from_q, from_v))
    at = lax.broadcasted_iota(jnp.int32, (BLK, 128), 1)
    small = jnp.zeros((BLK, 128), f32)
    for k, column in enumerate(columns):
        small = jnp.where(at == k, column, small)
    o_ref[:, 1024:1152] = small.astype(bf16)


def attn_grads(xhat, dq, dk, dv, d_mid0, d_mid1, context, packed, vectors):
    return kernel_call(
        attn_grads_body,
        (4,),
        [pl.BlockSpec((SEQ, BLK), lambda i: (0, i))]
        + [whole((SEQ, 256))] * 3
        + [pl.BlockSpec((HALF, BLK), lambda i: (0, i))] * 2
        + [
            whole((SEQ, 256)),
            rows(1152),
            pl.BlockSpec((8, BLK), lambda i: (0, i)),
            whole((8, D)),
        ],
        rows(1152),
        shape((D, 1152), bf16),
        2 * SEQ * D * D,
        scratch=[pltpu.VMEM((8, 768), f32)],
    )(xhat, dq, dk, dv, d_mid0, d_mid1, context, packed, vectors, vectors)


def input_grad_body(x_ref, a_ref, b_ref, c_ref, dm_ref, small_ref, o_ref):
    d_normed = a_ref[...].astype(f32) + b_ref[...].astype(f32) + c_ref[...].astype(f32)
    xhat, root = normalized(x_ref[...].astype(f32))
    o_ref[...] = dm_ref[...] + norm_pull(d_normed, xhat, root, small_ref[0:1, :])


def swap(values, axis):
    return lax.ppermute(values, axis, SWAP)


def sent_to_owners(grad):
    return lax.all_to_all(grad.reshape(16, 64, grad.shape[1]), XZ, 0, 0, tiled=True)


def summed(parts):
    total = jnp.sum(parts.astype(f32), axis=0)
    yl = lax.axis_index("yl")
    here = lax.dynamic_slice_in_dim(total, yl * 32, 32, 0)
    there = lax.dynamic_slice_in_dim(total, (1 - yl) * 32, 32, 0)
    return here + swap(there.astype(bf16), "yl").astype(f32)


def shards(
    tokens,
    cotangent,
    segments,
    ln1_gain,
    ln1_bias,
    w_qkv,
    bias_qv,
    w_out,
    bias_out,
    ln2_gain,
    ln2_bias,
    w_fc,
    bias_fc,
    w_proj,
    bias_proj,
):
    yh, core, yl = lax.axis_index("yh"), lax.axis_index("core"), lax.axis_index("yl")
    tiny = jnp.stack(
        [
            ln1_gain,
            ln1_bias,
            bias_out,
            ln2_gain,
            ln2_bias,
            bias_proj,
            jnp.pad(bias_qv.reshape(16), (0, 16)),
            bias_fc.reshape(32),
        ],
        axis=1,
    )
    pack = jnp.concatenate(
        [w_qkv.reshape(32, 768), w_out.T, jnp.pad(tiny, ((0, 0), (0, 120))), w_fc, w_proj.T],
        axis=1,
    )
    neighbour = swap(pack, "yl")
    both = jnp.where(
        yl == 0, jnp.concatenate([pack, neighbour]), jnp.concatenate([neighbour, pack])
    )
    packed_attn = lax.all_to_all(
        jnp.broadcast_to(both[:, :1152], (16, 64, 1152)), XZ, 0, 0, tiled=True
    ).reshape(D, 1152)
    small_t = packed_attn[:, 1024:1032].T
    at = jnp.arange(4, dtype=jnp.int32)
    loc = (at // 2 != yh).astype(jnp.int32) + 2 * (at % 2 != core).astype(jnp.int32)
    segc, segr = segments.reshape(SEQ, 1), segments.reshape(1, SEQ)
    x_mine = jnp.concatenate([tokens, swap(tokens, "yh")])
    x_all = jnp.concatenate([x_mine, swap(x_mine, "core")])
    second, small_t, x_all, segc = lax.optimization_barrier(
        (both[:, 1152:], small_t, x_all, segc)
    )
    packed = lax.all_gather(second, XZ, axis=0, tiled=True)

    smalls = small_t.astype(f32)
    qv = small_t[6].reshape(32, 32)[:, :16].reshape(32, 2, 4, 2).transpose(1, 2, 0, 3)
    qv = qv.reshape(2, 256).astype(f32)
    bias_row = jnp.concatenate([qv[0], jnp.zeros((256,), f32), qv[1]])[None]
    fc_bias = small_t[7].reshape(32, 8, 4).transpose(1, 0, 2).reshape(1, D).astype(f32)

    xhat_one, joined = qkv_rows(x_all, packed_attn, smalls, bias_row)
    joined, cot_late = lax.optimization_barrier((joined, cotangent))
    cot_mine = jnp.concatenate([cotangent, swap(cot_late, "yh")])
    cot_other = swap(cot_mine, "core")
    context = attend_forward(loc, segc, segr, joined)
    context, cot_mine = lax.optimization_barrier((context, cot_mine))
    received = swap(out_other(context, packed_attn), "core")
    s_out, out_here, out_there = out_mine(context, packed_attn, received)
    middle, n2_mine = middle_rows(
        x_mine, s_out, swap(out_there, "yh"), swap(out_here, "yh"), smalls
    )
    n2_other = swap(n2_mine, "core")

    act1, dh1, mlp1, dn1, sum1 = feed_other(n2_other, cot_other, packed, fc_bias)
    dn_in = swap(dn1, "core")
    act0, dh0, mlp0, s_dn, dn_here, dn_there, sum0 = feed_mine(
        n2_mine, cot_mine, packed, fc_bias, dn_in
    )
    from_there, from_here = swap(dn_there, "yh"), swap(dn_here, "yh")
    ff_grads = feed_grads(n2_mine, n2_other, dh0, dh1, cot_mine, cot_other, act0, act1)
    ff_grads, from_there = lax.optimization_barrier((ff_grads, from_there))
    ff_parts = sent_to_owners(ff_grads)
    d_middle, d_mid0, mid_sums = mid_grad(
        s_dn, from_there, from_here, middle, cot_mine, smalls
    )
    d_mid1 = swap(d_mid0, "core")
    d_context = context_grad(d_mid0, d_mid1, packed_attn)

    mlp1, _ = lax.optimization_barrier((mlp1, mid_sums))
    mlp_in = swap(mlp1, "core")
    mlp_there = (mlp0[BLK:] + mlp_in[BLK:].astype(f32)).astype(bf16)
    r_mlp = swap(mlp_there, "yh").astype(f32)
    mixed = (
        middle[:BLK] + (mlp0[:BLK] + mlp_in[:BLK].astype(f32) + r_mlp) + smalls[5:6]
    ).astype(bf16)
    vectors = jnp.concatenate([mid_sums[0:4], sum0[0:1] + sum1[0:1], mid_sums[5:8]])
    dq, dk, dv = attend_backward(loc, segc, segr, joined, d_context)
    grads = attn_grads(xhat_one, dq, dk, dv, d_mid0, d_mid1, context, packed_attn, vectors)
    grads, dq, dk, dv = lax.optimization_barrier((grads, dq, dk, dv))
    grads, ff_parts, mixed = lax.optimization_barrier((grads, ff_parts, mixed))
    grad_attn = summed(sent_to_owners(grads))
    grad_ff = summed(ff_parts)
    grad_fc, grad_proj = grad_ff[:, :D], grad_ff[:, D:].T
    grad_qkv, grad_out = grad_attn[:, :768].reshape(32, 3, 256), grad_attn[:, 768:1024].T
    d_n1 = norm_one_rows(dq, dk, dv, packed_attn)
    from_core = swap(d_n1[HALF:], "core")
    s_n1 = d_n1[BLK:HALF].astype(f32) + from_core[BLK:].astype(f32)
    from_far = swap(s_n1.astype(bf16), "yh")
    input_grad = kernel_call(
        input_grad_body,
        (1,),
        [whole((BLK, D))] * 5 + [whole((8, D))],
        whole((BLK, D)),
        shape((BLK, D), f32),
        BLK * D * 20,
    )(tokens, d_n1[:BLK], from_core[:BLK], from_far, d_middle[:BLK], smalls)

    small = grad_attn[:, 1024:1032]
    turned = [
        lax.ppermute(small, TP, [(k, (k + turn) % 4) for k in range(4)]) for turn in (1, 2, 3)
    ]
    everywhere = small + turned[0] + (turned[1] + turned[2])
    share = lax.dynamic_slice_in_dim(everywhere, 8 * (2 * yh + core), 8, 0)
    return (
        mixed,
        input_grad,
        share[:, 0],
        share[:, 1],
        grad_qkv,
        small[:16, 7].reshape(2, 4, 2),
        grad_out,
        everywhere[:, 5],
        share[:, 2],
        share[:, 3],
        grad_fc,
        small[:, 6].reshape(8, 4),
        grad_proj,
        everywhere[:, 4],
    )


def solution(mesh):
    fine = Mesh(mesh.devices.reshape(4, 4, 2, 2, 2), ALL)
    tok, dp, tp = P(ALL, None), DP, TP
    return jax.shard_map(
        shards,
        mesh=fine,
        in_specs=(
            tok,
            tok,
            P(dp),
            P(dp),
            P(dp),
            P(dp, None, tp),
            P(None, tp, dp),
            P(tp, dp),
            P(dp),
            P(dp),
            P(dp),
            P(dp, tp),
            P(tp, dp),
            P(tp, dp),
            P(dp),
        ),
        out_specs=(
            tok,
            tok,
            P(ALL),
            P(ALL),
            P(dp, None, tp),
            P(None, tp, dp),
            P(tp, dp),
            P(dp),
            P(ALL),
            P(ALL),
            P(dp, tp),
            P(tp, dp),
            P(tp, dp),
            P(dp),
        ),
        check_vma=False,
    )
```

```python
import functools

import jax
import jax.numpy as jnp
from jax import lax
from jax.experimental import pallas as pl
from jax.experimental.pallas import tpu as pltpu
from jax.sharding import Mesh
from jax.sharding import PartitionSpec as P

HD = 64
SEQ = 1024
D = 1024
BLK = 256
HALF = 512
EPS = 1e-05
GELU_C = 0.7978845608028654
GELU_A = 0.044715
DP = ("x", "z", "yl")
TP = ("yh", "core")
XZ = ("x", "z")
ALL = DP + TP
SWAP = [(0, 1), (1, 0)]
f32 = jnp.float32
bf16 = jnp.bfloat16
VMEM_BYTES = 32 * 1024 * 1024
VMEM_ALL = 62 * 1024 * 1024


def kernel_call(
    body, grid, in_specs, out_specs, out_shape, busy_us, prefetch=0, scratch=(), room=VMEM_BYTES
):
    return pl.pallas_call(
        body,
        out_shape=out_shape,
        grid_spec=pltpu.PrefetchScalarGridSpec(
            num_scalar_prefetch=prefetch,
            grid=grid,
            in_specs=in_specs,
            out_specs=out_specs,
            scratch_shapes=scratch,
        ),
        compiler_params=pltpu.CompilerParams(vmem_limit_bytes=room),
        cost_estimate=pl.CostEstimate(
            flops=int(busy_us * 1.15e9), bytes_accessed=int(busy_us * 3e6), transcendentals=0
        ),
    )


def shape(dims, dtype):
    return jax.ShapeDtypeStruct(dims, dtype)


def mm(a, b):
    return jnp.dot(a, b, preferred_element_type=f32)


def mm_nt(a, b):
    return lax.dot_general(a, b, (((1,), (1,)), ((), ())), preferred_element_type=f32)


def mm_tn(a, b):
    return lax.dot_general(a, b, (((0,), (0,)), ((), ())), preferred_element_type=f32)


def normalized(values):
    centered = values - jnp.mean(values, axis=-1, keepdims=True)
    variance = jnp.mean(centered * centered, axis=-1, keepdims=True)
    root = lax.rsqrt(variance + EPS)
    return centered * root, root


def norm_pull(grad, xhat, root, gain):
    scaled = grad * gain
    return root * (
        scaled
        - jnp.mean(scaled, axis=-1, keepdims=True)
        - xhat * jnp.mean(scaled * xhat, axis=-1, keepdims=True)
    )


def rows(width, move=lambda i: i, height=BLK):
    return pl.BlockSpec((height, width), lambda i, *_: (move(i), 0))


def whole(dims):
    return pl.BlockSpec(dims, lambda *_: (0,) * len(dims))


def picked(vector, lane):
    at = lax.broadcasted_iota(jnp.int32, (lane.shape[0], vector.shape[1]), 1)
    return jnp.sum(jnp.where(at == lane, vector.astype(f32), 0.0), axis=1, keepdims=True)


def side_columns(columns, height):
    at = lax.broadcasted_iota(jnp.int32, (height, 128), 1)
    small = jnp.zeros((height, 128), f32)
    for k, column in enumerate(columns):
        small = jnp.where(at == k, column, small)
    return small.astype(bf16)


def pack_body(*refs):
    vectors, (qv_ref, fc_ref, qkv_ref, out_ref, w_fc_ref, proj_ref, o_ref) = refs[:6], refs[6:]
    row = lax.broadcasted_iota(jnp.int32, (32, 1), 0)
    columns = [picked(ref[...], row) for ref in vectors]
    inner = row % 2
    qv = jnp.zeros((32, 1), f32)
    for s in range(2):
        for e in range(2):
            found = picked(qv_ref[s, e : e + 1, :], row % 8 // 2)
            qv = jnp.where((row // 8 == s) & (inner == e), found, qv)
    fc = jnp.zeros((32, 1), f32)
    for c in range(4):
        fc = jnp.where(row % 4 == c, picked(fc_ref[c : c + 1, :], row // 4), fc)
    for p in range(3):
        o_ref[:, p * 256 : (p + 1) * 256] = qkv_ref[p]
    o_ref[:, 768:1024] = out_ref[...]
    o_ref[:, 1024:1152] = side_columns(columns + [qv, fc], 32)
    o_ref[:, 1152:2176] = w_fc_ref[...]
    o_ref[:, 2176:3200] = proj_ref[...]


def packed_shards(vectors, bias_qv, bias_fc, w_qkv, w_out, w_fc, w_proj):
    arrays = [v.reshape(1, 32) for v in vectors] + [
        bias_qv.transpose(0, 2, 1),
        bias_fc.T,
        w_qkv.transpose(1, 0, 2),
        w_out.T,
        w_fc,
        w_proj.T,
    ]
    return kernel_call(
        pack_body,
        (1,),
        [whole(a.shape) for a in arrays],
        whole((32, 3200)),
        shape((32, 3200), bf16),
        2,
        room=VMEM_ALL,
    )(*arrays)


def small_out_body(t_ref, small_ref, a_ref, b_ref, c_ref, *outs):
    small = small_ref[...]
    total = small + a_ref[...] + (b_ref[...] + c_ref[...])

    def across(values, column, width, row_of):
        lane = lax.broadcasted_iota(jnp.int32, (32, width), 1)
        row = lax.broadcasted_iota(jnp.int32, (32, width), 0)
        found = jnp.where(row == row_of(lane), values[:, column : column + 1], 0.0)
        return jnp.sum(found, axis=0, keepdims=True)

    for k in range(4):
        outs[k][...] = across(total, k, 8, lambda lane: 8 * t_ref[0] + lane)
    for k in range(2):
        outs[4 + k][...] = across(total, 4 + k, 32, lambda lane: lane)
    for c in range(4):
        outs[6][c : c + 1, :] = across(small, 6, 8, lambda lane, c=c: 4 * lane + c)
    for s in range(2):
        for e in range(2):
            outs[7][s, e : e + 1, :] = across(
                small, 7, 4, lambda lane, s=s, e=e: 8 * s + 2 * lane + e
            )


def small_out(t, small, turned):
    dims = [(1, 8)] * 4 + [(1, 32)] * 2 + [(4, 8), (2, 2, 4)]
    return kernel_call(
        small_out_body,
        (1,),
        [whole((32, 8))] * 4,
        [whole(d) for d in dims],
        [shape(d, f32) for d in dims],
        1,
        prefetch=1,
        room=VMEM_ALL,
    )(t, small, *turned)


def qkv_body(x_ref, w_ref, small_ref, bias_ref, n_ref, j_ref):
    xhat, _ = normalized(x_ref[...].astype(f32))
    low = (xhat * small_ref[0:1, :] + small_ref[1:2, :]).astype(bf16)
    n_ref[...] = xhat.astype(bf16)
    j_ref[...] = (mm(low, w_ref[...]) + bias_ref[...]).astype(bf16)


def qkv_rows(x_all, packed, smalls, bias_row):
    return kernel_call(
        qkv_body,
        (4,),
        [rows(D), whole((D, 768)), whole((8, D)), whole((1, 768))],
        [rows(D), rows(768)],
        [shape((SEQ, D), bf16), shape((SEQ, 768), bf16)],
        4,
    )(x_all, packed, smalls, bias_row)


def allowed_block(segr_ref, s):
    width = (s + 1) * BLK
    row = lax.broadcasted_iota(jnp.int32, (BLK, 1), 0)
    same = picked(segr_ref[:, s * BLK : width], row) == segr_ref[:, :width]
    row_at = lax.broadcasted_iota(jnp.int32, (BLK, width), 0) + s * BLK
    key_at = lax.broadcasted_iota(jnp.int32, (BLK, width), 1)
    return same & (key_at <= row_at)


def place(loc_ref, s):
    return pl.ds(pl.multiple_of(loc_ref[s] * BLK, BLK), BLK)


def softmax_rows(scores, mask):
    scores = jnp.where(mask, scores, -1e30)
    highest = jnp.max(scores, axis=-1, keepdims=True)
    expanded = jnp.exp(scores - highest)
    return expanded * (1.0 / jnp.sum(expanded, axis=-1, keepdims=True))


def attend_body(loc_ref, segr_ref, q_ref, k_ref, v_ref, o_ref, kn, vn):
    first = lax.broadcasted_iota(jnp.int32, (1, 128), 1) < HD
    for s in range(4):
        kn[s * BLK : (s + 1) * BLK, :] = k_ref[place(loc_ref, s), :]
        vn[s * BLK : (s + 1) * BLK, :] = v_ref[place(loc_ref, s), :]
    for s in range(4):
        width = (s + 1) * BLK
        mask = allowed_block(segr_ref, s)
        q = q_ref[place(loc_ref, s), :] * jnp.asarray(HD**-0.5, bf16)
        done = []
        for mine in (first, ~first):
            qh = jnp.where(mine, q, jnp.zeros_like(q))
            probs = softmax_rows(mm_nt(qh, kn[:width, :]), mask).astype(bf16)
            done.append(mm(probs, vn[:width, :]))
        o_ref[place(loc_ref, s), :] = jnp.where(first, done[0], done[1]).astype(bf16)


def column_block(at):
    return pl.BlockSpec((SEQ, 128), lambda p, *_: (0, at + p))


def attend_forward(loc, segr, joined):
    return kernel_call(
        attend_body,
        (2,),
        [whole((1, SEQ)), column_block(0), column_block(2), column_block(4)],
        column_block(0),
        shape((SEQ, 256), bf16),
        9.5,
        prefetch=1,
        scratch=[pltpu.VMEM((SEQ, 128), bf16)] * 2,
    )(loc, segr, joined, joined, joined)


def attend_back_body(
    loc_ref, segr_ref, q_ref, k_ref, v_ref, d_ref, dq_ref, dk_ref, dv_ref, kn, vn, dk, dv
):
    first = lax.broadcasted_iota(jnp.int32, (1, 128), 1) < HD
    for s in range(4):
        kn[s * BLK : (s + 1) * BLK, :] = k_ref[place(loc_ref, s), :]
        vn[s * BLK : (s + 1) * BLK, :] = v_ref[place(loc_ref, s), :]
    for s in (3, 2, 1, 0):
        width = (s + 1) * BLK
        mask = allowed_block(segr_ref, s)
        q = q_ref[place(loc_ref, s), :] * jnp.asarray(HD**-0.5, bf16)
        d = d_ref[place(loc_ref, s), :]
        keys = kn[:width, :]
        values = vn[:width, :]
        dq_sum, dk_sum, dv_sum = [], [], []
        for mine in (first, ~first):
            qh = jnp.where(mine, q, jnp.zeros_like(q))
            dh = jnp.where(mine, d, jnp.zeros_like(d))
            probs = softmax_rows(mm_nt(qh, keys), mask)
            d_probs = mm_nt(dh, values)
            d_scores = (
                probs * (d_probs - jnp.sum(probs * d_probs, axis=-1, keepdims=True))
            ).astype(bf16)
            dq_sum.append(mm(d_scores, keys))
            dk_sum.append(mm_tn(d_scores, qh))
            dv_sum.append(mm_tn(probs.astype(bf16), dh))
        dq = jnp.where(first, dq_sum[0], dq_sum[1]) * (HD**-0.5)
        dq_ref[place(loc_ref, s), :] = dq.astype(bf16)
        if s == 3:
            dk[...] = dk_sum[0] + dk_sum[1]
            dv[...] = dv_sum[0] + dv_sum[1]
        else:
            dk[:width, :] += dk_sum[0] + dk_sum[1]
            dv[:width, :] += dv_sum[0] + dv_sum[1]
    for s in range(4):
        dk_ref[place(loc_ref, s), :] = dk[s * BLK : (s + 1) * BLK, :].astype(bf16)
        dv_ref[place(loc_ref, s), :] = dv[s * BLK : (s + 1) * BLK, :].astype(bf16)


def attend_backward(loc, segr, joined, d_context):
    return kernel_call(
        attend_back_body,
        (2,),
        [
            whole((1, SEQ)),
            column_block(0),
            column_block(2),
            column_block(4),
            column_block(0),
        ],
        [column_block(0)] * 3,
        [shape((SEQ, 256), bf16)] * 3,
        14,
        prefetch=1,
        scratch=[pltpu.VMEM((SEQ, 128), bf16)] * 2 + [pltpu.VMEM((SEQ, 128), f32)] * 2,
    )(loc, segr, joined, joined, joined, d_context)


def out_other_body(c_ref, w_ref, o_ref):
    o_ref[...] = mm_nt(c_ref[...], w_ref[...]).astype(bf16)


PART = whole((BLK, D))
THIN = rows(D, height=128)
OUT_COLUMNS = pl.BlockSpec((D, 256), lambda *_: (0, 3))
FC_COLUMNS = pl.BlockSpec((D, D), lambda *_: (0, 0))
PROJ_COLUMNS = pl.BlockSpec((D, D), lambda *_: (0, 1))


def out_other(context, packed):
    return kernel_call(
        out_other_body,
        (2,),
        [rows(256, lambda i: i + 2), OUT_COLUMNS],
        rows(D),
        shape((HALF, D), bf16),
        1.5,
    )(context, packed)


def out_mine_body(c_ref, w_ref, r_ref, p_ref, q_ref, p_low_ref, q_low_ref):
    total = mm_nt(c_ref[...], w_ref[...]) + r_ref[...].astype(f32)

    @pl.when(pl.program_id(0) == 0)
    def _():
        p_ref[...] = total
        p_low_ref[...] = total.astype(bf16)

    @pl.when(pl.program_id(0) == 1)
    def _():
        q_ref[...] = total
        q_low_ref[...] = total.astype(bf16)


def out_mine(context, packed, received):
    return kernel_call(
        out_mine_body,
        (2,),
        [rows(256), OUT_COLUMNS, rows(D)],
        [PART] * 4,
        [shape((BLK, D), f32)] * 2 + [shape((BLK, D), bf16)] * 2,
        2,
    )(context, packed, received)


def middle_body(x_ref, s_ref, r_ref, small_ref, mid_ref, n_ref):
    total = s_ref[...] + r_ref[...].astype(f32)
    middle = x_ref[...].astype(f32) + total + small_ref[2:3, :]
    mid_ref[...] = middle
    xhat, _ = normalized(middle)
    n_ref[...] = (xhat * small_ref[3:4, :] + small_ref[4:5, :]).astype(bf16)


def middle_rows(x, s, far, smalls):
    return kernel_call(
        middle_body,
        (2,),
        [THIN] * 3 + [whole((8, D))],
        [THIN] * 2,
        [shape((BLK, D), f32), shape((BLK, D), bf16)],
        1,
    )(x, s, far, smalls)


def feed_body(
    no_ref,
    nm_ref,
    go_ref,
    gm_ref,
    fc_ref,
    proj_ref,
    b_ref,
    a_ref,
    dh_ref,
    mo_ref,
    mm_ref,
    do_ref,
    dm_ref,
    sum_ref,
):
    other = pl.program_id(0) == 0
    n = jnp.where(other, no_ref[...], nm_ref[...])
    g = jnp.where(other, go_ref[...], gm_ref[...])

    @pl.when(other)
    def _():
        sum_ref[...] = jnp.zeros_like(sum_ref)

    for at in range(0, D, BLK):
        cut = slice(at, at + BLK)
        hidden = mm(n, fc_ref[:, cut]) + b_ref[:, cut]
        d_active = mm(g, proj_ref[:, cut])
        squared = hidden * hidden
        bent = jnp.tanh(hidden * (GELU_C + (GELU_A * GELU_C) * squared))
        half = 0.5 + 0.5 * bent
        slope = half + (0.5 * hidden) * (1.0 - bent * bent) * (
            GELU_C + (3.0 * GELU_A * GELU_C) * squared
        )
        d_hidden = (d_active * slope).astype(bf16)
        a_ref[:, cut] = (hidden * half).astype(bf16)
        dh_ref[:, cut] = d_hidden
        sum_ref[0:1, cut] += jnp.sum(d_hidden.astype(f32), axis=0, keepdims=True)
    d_normed = mm_nt(dh_ref[...], fc_ref[...])
    mixed = mm_nt(a_ref[...], proj_ref[...])

    @pl.when(other)
    def _():
        do_ref[...] = d_normed.astype(bf16)
        mo_ref[...] = mixed.astype(bf16)

    @pl.when(jnp.logical_not(other))
    def _():
        dm_ref[...] = d_normed
        mm_ref[...] = mixed


def feed(n_other, n_mine, g_other, g_mine, packed, fc_bias):
    return kernel_call(
        feed_body,
        (2,),
        [PART] * 4 + [FC_COLUMNS, PROJ_COLUMNS, whole((1, D))],
        [rows(D)] * 2 + [PART] * 4 + [whole((8, D))],
        [
            shape((HALF, D), bf16),
            shape((HALF, D), bf16),
            shape((BLK, D), bf16),
            shape((BLK, D), f32),
            shape((BLK, D), bf16),
            shape((BLK, D), f32),
            shape((8, D), f32),
        ],
        10,
        room=VMEM_ALL,
    )(n_other, n_mine, g_other, g_mine, packed, packed, fc_bias)


def feed_grad_body(r_ref, p_ref, s_ref, q_ref, hp_ref, hq_ref, o_ref):
    o_ref[...] = (
        mm_tn(r_ref[...], hp_ref[:BLK, :])
        + mm_tn(p_ref[...], hp_ref[BLK:, :])
        + mm_tn(s_ref[...], hq_ref[:BLK, :])
        + mm_tn(q_ref[...], hq_ref[BLK:, :])
    ).astype(bf16)


def feed_grad(r, p, s, q, by_p, by_q):
    part = pl.BlockSpec((BLK, BLK), lambda i: (0, i))
    return kernel_call(
        feed_grad_body,
        (4,),
        [part] * 4 + [whole((HALF, D))] * 2,
        rows(D),
        shape((D, D), bf16),
        4.5,
        room=VMEM_ALL,
    )(r, p, s, q, by_p, by_q)


def mid_grad_body(s_ref, r_ref, mid_ref, g_ref, small_ref, dm_ref, low_ref, sum_ref):
    d_normed = s_ref[...] + r_ref[...].astype(f32)
    xhat, root = normalized(mid_ref[...])
    g = g_ref[...].astype(f32)
    d_middle = g + norm_pull(d_normed, xhat, root, small_ref[3:4, :])
    dm_ref[...] = d_middle
    low = d_middle.astype(bf16)
    low_ref[...] = low

    @pl.when(pl.program_id(0) == 0)
    def _():
        sum_ref[...] = jnp.zeros_like(sum_ref)

    sum_ref[0:1, :] += 0.5 * jnp.sum(d_normed * xhat, axis=0, keepdims=True)
    sum_ref[1:2, :] += 0.5 * jnp.sum(d_normed, axis=0, keepdims=True)
    sum_ref[2:3, :] += 0.5 * jnp.sum(g, axis=0, keepdims=True)
    sum_ref[3:4, :] += 0.5 * jnp.sum(low.astype(f32), axis=0, keepdims=True)


def mid_grad(s, far, middle, cot, smalls):
    return kernel_call(
        mid_grad_body,
        (2,),
        [THIN] * 4 + [whole((8, D))],
        [THIN] * 2 + [whole((8, D))],
        [shape((BLK, D), f32), shape((BLK, D), bf16), shape((8, D), f32)],
        2,
    )(s, far, middle, cot, smalls)


def context_grad_body(p_ref, q_ref, r_ref, s_ref, w_ref, o_ref):
    for k, ref in enumerate((p_ref, q_ref, r_ref, s_ref)):
        o_ref[k * BLK : (k + 1) * BLK, :] = mm(ref[...], w_ref[...]).astype(bf16)


def context_grad(parts, packed):
    return kernel_call(
        context_grad_body,
        (1,),
        [PART] * 4 + [OUT_COLUMNS],
        whole((SEQ, 256)),
        shape((SEQ, 256), bf16),
        1,
    )(*parts, packed)


def norm_one_part(q_ref, k_ref, v_ref, w_ref):
    return (
        mm_nt(q_ref[...], w_ref[:, :256])
        + mm_nt(k_ref[...], w_ref[:, 256:512])
        + mm_nt(v_ref[...], w_ref[:, 512:768])
    )


def norm_one_other_body(q_ref, k_ref, v_ref, w_ref, o_ref):
    o_ref[...] = norm_one_part(q_ref, k_ref, v_ref, w_ref).astype(bf16)


def norm_one_other(dq, dk, dv, packed):
    return kernel_call(
        norm_one_other_body,
        (2,),
        [rows(256, lambda i: i + 2)] * 3 + [whole((D, 768))],
        rows(D),
        shape((HALF, D), bf16),
        2,
    )(dq, dk, dv, packed)


def norm_one_mine_body(h_ref, q_ref, k_ref, v_ref, w_ref, r_ref, here_ref, there_ref):
    total = norm_one_part(q_ref, k_ref, v_ref, w_ref) + r_ref[...].astype(f32)

    @pl.when(pl.program_id(0) == 0)
    def _():
        there_ref[...] = total.astype(bf16)

    @pl.when(pl.program_id(0) == 1)
    def _():
        here_ref[...] = total


def norm_one_mine(h, dq, dk, dv, packed, received):
    def turned(width):
        return pl.BlockSpec((BLK, width), lambda i, h_ref: (jnp.where(i == 1, h_ref[0], 1 - h_ref[0]), 0))

    return kernel_call(
        norm_one_mine_body,
        (2,),
        [turned(256)] * 3 + [whole((D, 768)), turned(D)],
        [PART] * 2,
        [shape((BLK, D), f32), shape((BLK, D), bf16)],
        3,
        prefetch=1,
    )(h, dq, dk, dv, packed, received)


def attn_grads_body(
    n_ref, q_ref, k_ref, v_ref, mp_ref, mq_ref, mr_ref, ms_ref, c_ref, w_ref, vp_ref, vq_ref, f0_ref, f1_ref, o_ref, sums
):
    step = pl.program_id(0)

    @pl.when(step == 0)
    def _():
        for p, ref in enumerate((q_ref, k_ref, v_ref)):
            sums[0:1, p * 256 : (p + 1) * 256] = jnp.sum(
                ref[...].astype(f32), axis=0, keepdims=True
            )

    n = n_ref[...]
    gain = w_ref[:, 1024:1025].astype(f32)
    offset = w_ref[:, 1025:1026].astype(f32)
    by_gain = jnp.zeros((BLK, 1), f32)
    by_bias = jnp.zeros((BLK, 1), f32)
    for p, ref in enumerate((q_ref, k_ref, v_ref)):
        cut = slice(p * 256, (p + 1) * 256)
        raw = mm_tn(n, ref[...])
        total = sums[0:1, cut]
        weight = w_ref[:, cut].astype(f32)
        by_gain += jnp.sum(weight * raw, axis=1, keepdims=True)
        by_bias += jnp.sum(weight * total, axis=1, keepdims=True)
        o_ref[:, cut] = (raw * gain + offset * total).astype(bf16)
    out = jnp.zeros((BLK, 256), f32)
    for k, ref in enumerate((mp_ref, mq_ref, mr_ref, ms_ref)):
        out += mm_tn(ref[...], c_ref[k * BLK : (k + 1) * BLK, :])
    o_ref[:, 768:1024] = out.astype(bf16)
    row = lax.broadcasted_iota(jnp.int32, (BLK, 1), 0)
    owner, inner = step * (BLK // 32) + row // 32, row % 32
    columns = [by_gain, by_bias] + [
        picked(vp_ref[k : k + 1, :] + vq_ref[k : k + 1, :], row) for k in range(4)
    ]
    columns.append(picked(f0_ref[0:1, :] + f1_ref[0:1, :], inner // 4 * 128 + owner * 4 + inner % 4))
    lane = inner % 8 // 2 * HD + owner * 2 + inner % 2
    from_q = picked(sums[0:1, 0:256], lane)
    from_v = picked(sums[0:1, 512:768], lane)
    columns.append(jnp.where(inner < 8, from_q, from_v))
    o_ref[:, 1024:1152] = side_columns(columns, BLK)


def attn_grads(xhat, dq, dk, dv, d_mids, context, packed, sums_p, sums_q, fc0, fc1):
    return kernel_call(
        attn_grads_body,
        (4,),
        [pl.BlockSpec((SEQ, BLK), lambda i: (0, i))]
        + [whole((SEQ, 256))] * 3
        + [pl.BlockSpec((BLK, BLK), lambda i: (0, i))] * 4
        + [whole((SEQ, 256)), rows(1152)]
        + [pl.BlockSpec((8, BLK), lambda i: (0, i))] * 2
        + [whole((8, D))] * 2,
        rows(1152),
        shape((D, 1152), bf16),
        6.5,
        scratch=[pltpu.VMEM((8, 768), f32)],
    )(xhat, dq, dk, dv, *d_mids, context, packed, sums_p, sums_q, fc0, fc1)


def input_grad_body(x_ref, a_ref, b_ref, dm_ref, small_ref, o_ref):
    d_normed = a_ref[...] + b_ref[...].astype(f32)
    xhat, root = normalized(x_ref[...].astype(f32))
    o_ref[...] = dm_ref[...] + norm_pull(d_normed, xhat, root, small_ref[0:1, :])


def input_grad_rows(tokens, here, far, d_middle, smalls):
    return kernel_call(
        input_grad_body,
        (2,),
        [THIN] * 4 + [whole((8, D))],
        THIN,
        shape((BLK, D), f32),
        1.5,
    )(tokens, here, far, d_middle, smalls)


def swap(values, axis):
    return lax.ppermute(values, axis, SWAP)


def sent_to_owners(grad):
    return lax.all_to_all(grad.reshape(16, 64, grad.shape[1]), XZ, 0, 0, tiled=True)


def owned(total):
    yl = lax.axis_index("yl")
    here = lax.dynamic_slice_in_dim(total, yl * 32, 32, 0)
    there = lax.dynamic_slice_in_dim(total, (1 - yl) * 32, 32, 0)
    return here + swap(there.astype(bf16), "yl").astype(f32)


def shards(
    tokens,
    cotangent,
    segments,
    ln1_gain,
    ln1_bias,
    w_qkv,
    bias_qv,
    w_out,
    bias_out,
    ln2_gain,
    ln2_bias,
    w_fc,
    bias_fc,
    w_proj,
    bias_proj,
):
    yh, core, yl = lax.axis_index("yh"), lax.axis_index("core"), lax.axis_index("yl")
    pack = packed_shards(
        [ln1_gain, ln1_bias, bias_out, ln2_gain, ln2_bias, bias_proj],
        bias_qv,
        bias_fc,
        w_qkv,
        w_out,
        w_fc,
        w_proj,
    )
    pack, tokens_late = lax.optimization_barrier((pack, tokens))
    neighbour = swap(pack, "yl")
    both = jnp.where(
        yl == 0, jnp.concatenate([pack, neighbour]), jnp.concatenate([neighbour, pack])
    )
    at = jnp.arange(4, dtype=jnp.int32)
    loc = at // 2 + 2 * (at % 2 != core).astype(jnp.int32)

    def by_half(own, far):
        return jnp.where(yh == 0, own, far), jnp.where(yh == 0, far, own)

    segr = segments.reshape(1, SEQ).astype(f32)
    packed_attn = lax.all_to_all(
        jnp.broadcast_to(both[:, :1152], (16, 64, 1152)), XZ, 0, 0, tiled=True
    ).reshape(D, 1152)
    x_p, x_q = by_half(tokens, swap(tokens_late, "yh"))
    x_mine = jnp.concatenate([x_p, x_q])
    x_all = jnp.concatenate([x_mine, swap(x_mine, "core")])
    small_t = packed_attn[:, 1024:1032].T
    second, small_t, x_all = lax.optimization_barrier((both[:, 1152:], small_t, x_all))
    packed = lax.all_gather(second, XZ, axis=0, tiled=True)

    smalls = small_t.astype(f32)
    qv = small_t[6].reshape(32, 32)[:, :16].reshape(32, 2, 4, 2).transpose(1, 2, 0, 3)
    qv = qv.reshape(2, 256).astype(f32)
    bias_row = jnp.concatenate([qv[0], jnp.zeros((256,), f32), qv[1]])[None]
    fc_bias = small_t[7].reshape(32, 8, 4).transpose(1, 0, 2).reshape(1, D).astype(f32)

    xhat_one, joined = qkv_rows(x_all, packed_attn, smalls, bias_row)
    joined, cot_late = lax.optimization_barrier((joined, cotangent))
    c_p, c_q = by_half(cotangent, swap(cot_late, "yh"))
    context = attend_forward(loc, segr, joined)
    context, c_p, c_q = lax.optimization_barrier((context, c_p, c_q))
    c_r, c_s = swap(c_p, "core"), swap(c_q, "core")
    received = swap(out_other(context, packed_attn), "core")
    s_p, s_q, low_p, low_q = out_mine(context, packed_attn, received)
    far_p, far_q = swap(low_p, "yh"), swap(low_q, "yh")
    far_p, fc_bias = lax.optimization_barrier((far_p, fc_bias))

    mid_p, n_p = middle_rows(x_p, s_p, far_p, smalls)
    n_r = swap(n_p, "core")
    act_p, dh_p, mo_p, mm_p, do_p, dm_p, sum_p = feed(n_r, n_p, c_r, c_p, packed, fc_bias)
    do_p, far_q = lax.optimization_barrier((do_p, far_q))
    mid_q, n_q = middle_rows(x_q, s_q, far_q, smalls)
    n_s = swap(n_q, "core")
    dn_p = dm_p + swap(do_p, "core").astype(f32)
    dn_p_low, n_q = lax.optimization_barrier((dn_p.astype(bf16), n_q))
    r_p = swap(dn_p_low, "yh")
    act_q, dh_q, mo_q, mm_q, do_q, dm_q, sum_q = feed(n_s, n_q, c_s, c_q, packed, fc_bias)
    mo_q, r_p = lax.optimization_barrier((mo_q, r_p))
    dn_q = dm_q + swap(do_q, "core").astype(f32)
    r_q = swap(dn_q.astype(bf16), "yh")
    grads_fc = feed_grad(n_r, n_p, n_s, n_q, dh_p, dh_q)
    grads_proj = feed_grad(c_r, c_p, c_s, c_q, act_p, act_q)
    dmid_p, dl_p, vec_p = mid_grad(dn_p, r_p, mid_p, c_p, smalls)
    dl_p, r_q = lax.optimization_barrier((dl_p, r_q))
    dl_r = swap(dl_p, "core")
    grads_fc, grads_proj, r_q = lax.optimization_barrier((grads_fc, grads_proj, r_q))
    fc_share = lax.psum_scatter(grads_fc, "x", scatter_dimension=0, tiled=True)
    fc_share = lax.psum_scatter(fc_share, "z", scatter_dimension=0, tiled=True)
    proj_parts = sent_to_owners(grads_proj)
    dmid_q, dl_q, vec_q = mid_grad(dn_q, r_q, mid_q, c_q, smalls)
    dl_s = swap(dl_q, "core")
    d_mids = (dl_p, dl_q, dl_r, dl_s)
    d_context = context_grad(d_mids, packed_attn)

    mo_p, mo_q, _ = lax.optimization_barrier((mo_p, mo_q, vec_q))
    mlp_p = mm_p + swap(mo_p, "core").astype(f32)
    mlp_q = mm_q + swap(mo_q, "core").astype(f32)
    mlp_own, mlp_far = by_half(mlp_p, mlp_q)
    mid_own, _ = by_half(mid_p, mid_q)
    r_mlp = swap(mlp_far.astype(bf16), "yh")
    dmid_own, _ = by_half(dmid_p, dmid_q)

    dq, dk, dv = attend_backward(loc, segr, joined, d_context)
    grads = attn_grads(
        xhat_one, dq, dk, dv, d_mids, context, packed_attn, vec_p, vec_q, sum_p, sum_q
    )
    grads, dq, dk, dv = lax.optimization_barrier((grads, dq, dk, dv))
    grads, r_mlp, proj_parts = lax.optimization_barrier((grads, r_mlp, proj_parts))
    mixed = (mid_own + (mlp_own + r_mlp.astype(f32)) + smalls[5:6]).astype(bf16)
    parts = sent_to_owners(grads)
    grad_attn = owned(jnp.sum(parts.astype(f32), axis=0))
    grad_fc = owned(fc_share.astype(f32))
    grad_proj = owned(jnp.sum(proj_parts.astype(f32), axis=0)).T
    grad_qkv, grad_out = grad_attn[:, :768].reshape(32, 3, 256), grad_attn[:, 768:1024].T
    from_core = swap(norm_one_other(dq, dk, dv, packed_attn), "core")
    d_here, d_there = norm_one_mine(
        yh.astype(jnp.int32).reshape(1), dq, dk, dv, packed_attn, from_core
    )
    input_grad = input_grad_rows(tokens, d_here, swap(d_there, "yh"), dmid_own, smalls)

    small = grad_attn[:, 1024:1032]
    turned = [
        lax.ppermute(small, TP, [(k, (k + turn) % 4) for k in range(4)]) for turn in (1, 2, 3)
    ]
    t = (2 * yh + core).astype(jnp.int32).reshape(1)
    outs = small_out(t, small, turned)
    return (
        mixed,
        input_grad,
        outs[0].reshape(8),
        outs[1].reshape(8),
        grad_qkv,
        outs[7].transpose(0, 2, 1),
        grad_out,
        outs[5].reshape(32),
        outs[2].reshape(8),
        outs[3].reshape(8),
        grad_fc,
        outs[6].T,
        grad_proj,
        outs[4].reshape(32),
    )


def solution(mesh):
    fine = Mesh(mesh.devices.reshape(4, 4, 2, 2, 2), ALL)
    tok, dp, tp = P(ALL, None), DP, TP
    return jax.shard_map(
        shards,
        mesh=fine,
        in_specs=(
            tok,
            tok,
            P(dp),
            P(dp),
            P(dp),
            P(dp, None, tp),
            P(None, tp, dp),
            P(tp, dp),
            P(dp),
            P(dp),
            P(dp),
            P(dp, tp),
            P(tp, dp),
            P(tp, dp),
            P(dp),
        ),
        out_specs=(
            tok,
            tok,
            P(ALL),
            P(ALL),
            P(dp, None, tp),
            P(None, tp, dp),
            P(tp, dp),
            P(dp),
            P(ALL),
            P(ALL),
            P(dp, tp),
            P(tp, dp),
            P(tp, dp),
            P(dp),
        ),
        check_vma=False,
    )
```

```python
import functools

import jax
import jax.numpy as jnp
from jax import lax
from jax.experimental import pallas as pl
from jax.experimental.pallas import tpu as pltpu
from jax.sharding import Mesh
from jax.sharding import PartitionSpec as P

HD = 64
SEQ = 1024
D = 1024
BLK = 256
HALF = 512
EPS = 1e-05
GELU_C = 0.7978845608028654
GELU_A = 0.044715
DP = ("x", "z", "yl")
TP = ("yh", "core")
XZ = ("x", "z")
ALL = DP + TP
SWAP = [(0, 1), (1, 0)]
f32 = jnp.float32
bf16 = jnp.bfloat16
VMEM_BYTES = 32 * 1024 * 1024
VMEM_ALL = 62 * 1024 * 1024


def kernel_call(
    body, grid, in_specs, out_specs, out_shape, busy_us, prefetch=0, scratch=(), room=VMEM_BYTES
):
    return pl.pallas_call(
        body,
        out_shape=out_shape,
        grid_spec=pltpu.PrefetchScalarGridSpec(
            num_scalar_prefetch=prefetch,
            grid=grid,
            in_specs=in_specs,
            out_specs=out_specs,
            scratch_shapes=scratch,
        ),
        compiler_params=pltpu.CompilerParams(vmem_limit_bytes=room),
        cost_estimate=pl.CostEstimate(
            flops=int(busy_us * 1.15e9), bytes_accessed=int(busy_us * 3e6), transcendentals=0
        ),
    )


def shape(dims, dtype):
    return jax.ShapeDtypeStruct(dims, dtype)


def mm(a, b):
    return jnp.dot(a, b, preferred_element_type=f32)


def mm_nt(a, b):
    return lax.dot_general(a, b, (((1,), (1,)), ((), ())), preferred_element_type=f32)


def mm_tn(a, b):
    return lax.dot_general(a, b, (((0,), (0,)), ((), ())), preferred_element_type=f32)


def normalized(values):
    centered = values - jnp.mean(values, axis=-1, keepdims=True)
    variance = jnp.mean(centered * centered, axis=-1, keepdims=True)
    root = lax.rsqrt(variance + EPS)
    return centered * root, root


def norm_pull(grad, xhat, root, gain):
    scaled = grad * gain
    return root * (
        scaled
        - jnp.mean(scaled, axis=-1, keepdims=True)
        - xhat * jnp.mean(scaled * xhat, axis=-1, keepdims=True)
    )


def rows(width, move=lambda i: i, height=BLK):
    return pl.BlockSpec((height, width), lambda i, *_: (move(i), 0))


def whole(dims):
    return pl.BlockSpec(dims, lambda *_: (0,) * len(dims))


def picked(vector, lane):
    at = lax.broadcasted_iota(jnp.int32, (lane.shape[0], vector.shape[1]), 1)
    return jnp.sum(jnp.where(at == lane, vector.astype(f32), 0.0), axis=1, keepdims=True)


def side_columns(columns, height):
    at = lax.broadcasted_iota(jnp.int32, (height, 128), 1)
    small = jnp.zeros((height, 128), f32)
    for k, column in enumerate(columns):
        small = jnp.where(at == k, column, small)
    return small.astype(bf16)


def pack_body(*refs):
    vectors, (qv_ref, fc_ref, qkv_ref, out_ref, w_fc_ref, proj_ref, o_ref) = refs[:6], refs[6:]
    row = lax.broadcasted_iota(jnp.int32, (32, 1), 0)
    columns = [picked(ref[...], row) for ref in vectors]
    inner = row % 2
    qv = jnp.zeros((32, 1), f32)
    for s in range(2):
        for e in range(2):
            found = picked(qv_ref[s, e : e + 1, :], row % 8 // 2)
            qv = jnp.where((row // 8 == s) & (inner == e), found, qv)
    fc = jnp.zeros((32, 1), f32)
    for c in range(4):
        fc = jnp.where(row % 4 == c, picked(fc_ref[c : c + 1, :], row // 4), fc)
    for p in range(3):
        o_ref[:, p * 256 : (p + 1) * 256] = qkv_ref[p]
    o_ref[:, 768:1024] = out_ref[...]
    o_ref[:, 1024:1152] = side_columns(columns + [qv, fc], 32)
    o_ref[:, 1152:2176] = w_fc_ref[...]
    o_ref[:, 2176:3200] = proj_ref[...]


def packed_shards(vectors, bias_qv, bias_fc, w_qkv, w_out, w_fc, w_proj):
    arrays = [v.reshape(1, 32) for v in vectors] + [
        bias_qv.transpose(0, 2, 1),
        bias_fc.T,
        w_qkv.transpose(1, 0, 2),
        w_out.T,
        w_fc,
        w_proj.T,
    ]
    return kernel_call(
        pack_body,
        (1,),
        [whole(a.shape) for a in arrays],
        whole((32, 3200)),
        shape((32, 3200), bf16),
        2,
        room=VMEM_ALL,
    )(*arrays)


def small_out_body(t_ref, small_ref, a_ref, b_ref, c_ref, *outs):
    small = small_ref[...]
    total = small + a_ref[...] + (b_ref[...] + c_ref[...])

    def across(values, column, width, row_of):
        lane = lax.broadcasted_iota(jnp.int32, (32, width), 1)
        row = lax.broadcasted_iota(jnp.int32, (32, width), 0)
        found = jnp.where(row == row_of(lane), values[:, column : column + 1], 0.0)
        return jnp.sum(found, axis=0, keepdims=True)

    for k in range(4):
        outs[k][...] = across(total, k, 8, lambda lane: 8 * t_ref[0] + lane)
    for k in range(2):
        outs[4 + k][...] = across(total, 4 + k, 32, lambda lane: lane)
    for c in range(4):
        outs[6][c : c + 1, :] = across(small, 6, 8, lambda lane, c=c: 4 * lane + c)
    for s in range(2):
        for e in range(2):
            outs[7][s, e : e + 1, :] = across(
                small, 7, 4, lambda lane, s=s, e=e: 8 * s + 2 * lane + e
            )


def small_out(t, small, turned):
    dims = [(1, 8)] * 4 + [(1, 32)] * 2 + [(4, 8), (2, 2, 4)]
    return kernel_call(
        small_out_body,
        (1,),
        [whole((32, 8))] * 4,
        [whole(d) for d in dims],
        [shape(d, f32) for d in dims],
        1,
        prefetch=1,
        room=VMEM_ALL,
    )(t, small, *turned)


def qkv_body(x_ref, w_ref, small_ref, bias_ref, n_ref, j_ref):
    xhat, _ = normalized(x_ref[...].astype(f32))
    low = (xhat * small_ref[0:1, :] + small_ref[1:2, :]).astype(bf16)
    n_ref[...] = xhat.astype(bf16)
    j_ref[...] = (mm(low, w_ref[...]) + bias_ref[...]).astype(bf16)


def qkv_rows(x_all, packed, smalls, bias_row):
    return kernel_call(
        qkv_body,
        (4,),
        [rows(D), whole((D, 768)), whole((8, D)), whole((1, 768))],
        [rows(D), rows(768)],
        [shape((SEQ, D), bf16), shape((SEQ, 768), bf16)],
        4,
    )(x_all, packed, smalls, bias_row)


def allowed_block(segr_ref, s):
    width = (s + 1) * BLK
    row = lax.broadcasted_iota(jnp.int32, (BLK, 1), 0)
    same = picked(segr_ref[:, s * BLK : width], row) == segr_ref[:, :width]
    row_at = lax.broadcasted_iota(jnp.int32, (BLK, width), 0) + s * BLK
    key_at = lax.broadcasted_iota(jnp.int32, (BLK, width), 1)
    return same & (key_at <= row_at)


def place(loc_ref, s):
    return pl.ds(pl.multiple_of(loc_ref[s] * BLK, BLK), BLK)


def softmax_rows(scores, mask):
    scores = jnp.where(mask, scores, -1e30)
    highest = jnp.max(scores, axis=-1, keepdims=True)
    expanded = jnp.exp(scores - highest)
    return expanded * (1.0 / jnp.sum(expanded, axis=-1, keepdims=True))


def attend_body(loc_ref, segr_ref, q_ref, k_ref, v_ref, o_ref, kn, vn):
    first = lax.broadcasted_iota(jnp.int32, (1, 128), 1) < HD
    for s in range(4):
        kn[s * BLK : (s + 1) * BLK, :] = k_ref[place(loc_ref, s), :]
        vn[s * BLK : (s + 1) * BLK, :] = v_ref[place(loc_ref, s), :]
    for s in range(4):
        width = (s + 1) * BLK
        mask = allowed_block(segr_ref, s)
        q = q_ref[place(loc_ref, s), :] * jnp.asarray(HD**-0.5, bf16)
        done = []
        for mine in (first, ~first):
            qh = jnp.where(mine, q, jnp.zeros_like(q))
            probs = softmax_rows(mm_nt(qh, kn[:width, :]), mask).astype(bf16)
            done.append(mm(probs, vn[:width, :]))
        o_ref[place(loc_ref, s), :] = jnp.where(first, done[0], done[1]).astype(bf16)


def column_block(at):
    return pl.BlockSpec((SEQ, 128), lambda p, *_: (0, at + p))


def attend_forward(loc, segr, joined):
    return kernel_call(
        attend_body,
        (2,),
        [whole((1, SEQ)), column_block(0), column_block(2), column_block(4)],
        column_block(0),
        shape((SEQ, 256), bf16),
        9.5,
        prefetch=1,
        scratch=[pltpu.VMEM((SEQ, 128), bf16)] * 2,
    )(loc, segr, joined, joined, joined)


def attend_back_body(
    loc_ref, segr_ref, q_ref, k_ref, v_ref, d_ref, dq_ref, dk_ref, dv_ref, kn, vn, dk, dv
):
    first = lax.broadcasted_iota(jnp.int32, (1, 128), 1) < HD
    for s in range(4):
        kn[s * BLK : (s + 1) * BLK, :] = k_ref[place(loc_ref, s), :]
        vn[s * BLK : (s + 1) * BLK, :] = v_ref[place(loc_ref, s), :]
    for s in (3, 2, 1, 0):
        width = (s + 1) * BLK
        mask = allowed_block(segr_ref, s)
        q = q_ref[place(loc_ref, s), :] * jnp.asarray(HD**-0.5, bf16)
        d = d_ref[place(loc_ref, s), :]
        keys = kn[:width, :]
        values = vn[:width, :]
        dq_sum, dk_sum, dv_sum = [], [], []
        for mine in (first, ~first):
            qh = jnp.where(mine, q, jnp.zeros_like(q))
            dh = jnp.where(mine, d, jnp.zeros_like(d))
            probs = softmax_rows(mm_nt(qh, keys), mask)
            d_probs = mm_nt(dh, values)
            d_scores = (
                probs * (d_probs - jnp.sum(probs * d_probs, axis=-1, keepdims=True))
            ).astype(bf16)
            dq_sum.append(mm(d_scores, keys))
            dk_sum.append(mm_tn(d_scores, qh))
            dv_sum.append(mm_tn(probs.astype(bf16), dh))
        dq = jnp.where(first, dq_sum[0], dq_sum[1]) * (HD**-0.5)
        dq_ref[place(loc_ref, s), :] = dq.astype(bf16)
        if s == 3:
            dk[...] = dk_sum[0] + dk_sum[1]
            dv[...] = dv_sum[0] + dv_sum[1]
        else:
            dk[:width, :] += dk_sum[0] + dk_sum[1]
            dv[:width, :] += dv_sum[0] + dv_sum[1]
    for s in range(4):
        dk_ref[place(loc_ref, s), :] = dk[s * BLK : (s + 1) * BLK, :].astype(bf16)
        dv_ref[place(loc_ref, s), :] = dv[s * BLK : (s + 1) * BLK, :].astype(bf16)


def attend_backward(loc, segr, joined, d_context):
    return kernel_call(
        attend_back_body,
        (2,),
        [
            whole((1, SEQ)),
            column_block(0),
            column_block(2),
            column_block(4),
            column_block(0),
        ],
        [column_block(0)] * 3,
        [shape((SEQ, 256), bf16)] * 3,
        14,
        prefetch=1,
        scratch=[pltpu.VMEM((SEQ, 128), bf16)] * 2 + [pltpu.VMEM((SEQ, 128), f32)] * 2,
    )(loc, segr, joined, joined, joined, d_context)


def out_other_body(c_ref, w_ref, o_ref):
    o_ref[...] = mm_nt(c_ref[...], w_ref[...]).astype(bf16)


PART = whole((BLK, D))
THIN = rows(D, height=128)
OUT_COLUMNS = pl.BlockSpec((D, 256), lambda *_: (0, 3))
FC_COLUMNS = pl.BlockSpec((D, D), lambda *_: (0, 0))
PROJ_COLUMNS = pl.BlockSpec((D, D), lambda *_: (0, 1))


def out_other(context, packed):
    return kernel_call(
        out_other_body,
        (2,),
        [rows(256, lambda i: i + 2), OUT_COLUMNS],
        rows(D),
        shape((HALF, D), bf16),
        1.5,
    )(context, packed)


def out_mine_body(c_ref, w_ref, r_ref, p_ref, q_ref, p_low_ref, q_low_ref):
    total = mm_nt(c_ref[...], w_ref[...]) + r_ref[...].astype(f32)

    @pl.when(pl.program_id(0) == 0)
    def _():
        p_ref[...] = total
        p_low_ref[...] = total.astype(bf16)

    @pl.when(pl.program_id(0) == 1)
    def _():
        q_ref[...] = total
        q_low_ref[...] = total.astype(bf16)


def out_mine(context, packed, received):
    return kernel_call(
        out_mine_body,
        (2,),
        [rows(256), OUT_COLUMNS, rows(D)],
        [PART] * 4,
        [shape((BLK, D), f32)] * 2 + [shape((BLK, D), bf16)] * 2,
        2,
        room=VMEM_ALL,
    )(context, packed, received)


def middle_body(x_ref, s_ref, r_ref, small_ref, mid_ref, n_ref):
    total = s_ref[...] + r_ref[...].astype(f32)
    middle = x_ref[...].astype(f32) + total + small_ref[2:3, :]
    mid_ref[...] = middle
    xhat, _ = normalized(middle)
    n_ref[...] = (xhat * small_ref[3:4, :] + small_ref[4:5, :]).astype(bf16)


def middle_rows(x, s, far, smalls):
    return kernel_call(
        middle_body,
        (2,),
        [THIN] * 3 + [whole((8, D))],
        [THIN] * 2,
        [shape((BLK, D), f32), shape((BLK, D), bf16)],
        1,
    )(x, s, far, smalls)


def feed_body(
    no_ref,
    nm_ref,
    go_ref,
    gm_ref,
    fc_ref,
    proj_ref,
    b_ref,
    a_ref,
    dh_ref,
    mo_ref,
    mm_ref,
    do_ref,
    dm_ref,
    sum_ref,
):
    other = pl.program_id(0) == 0
    n = jnp.where(other, no_ref[...], nm_ref[...])
    g = jnp.where(other, go_ref[...], gm_ref[...])

    @pl.when(other)
    def _():
        sum_ref[...] = jnp.zeros_like(sum_ref)

    for at in range(0, D, BLK):
        cut = slice(at, at + BLK)
        hidden = mm(n, fc_ref[:, cut]) + b_ref[:, cut]
        d_active = mm(g, proj_ref[:, cut])
        squared = hidden * hidden
        bent = jnp.tanh(hidden * (GELU_C + (GELU_A * GELU_C) * squared))
        half = 0.5 + 0.5 * bent
        slope = half + (0.5 * hidden) * (1.0 - bent * bent) * (
            GELU_C + (3.0 * GELU_A * GELU_C) * squared
        )
        d_hidden = (d_active * slope).astype(bf16)
        a_ref[:, cut] = (hidden * half).astype(bf16)
        dh_ref[:, cut] = d_hidden
        sum_ref[0:1, cut] += jnp.sum(d_hidden.astype(f32), axis=0, keepdims=True)
    d_normed = mm_nt(dh_ref[...], fc_ref[...])
    mixed = mm_nt(a_ref[...], proj_ref[...])

    @pl.when(other)
    def _():
        do_ref[...] = d_normed.astype(bf16)
        mo_ref[...] = mixed.astype(bf16)

    @pl.when(jnp.logical_not(other))
    def _():
        dm_ref[...] = d_normed
        mm_ref[...] = mixed


def feed(n_other, n_mine, g_other, g_mine, packed, fc_bias):
    return kernel_call(
        feed_body,
        (2,),
        [PART] * 4 + [FC_COLUMNS, PROJ_COLUMNS, whole((1, D))],
        [rows(D)] * 2 + [PART] * 4 + [whole((8, D))],
        [
            shape((HALF, D), bf16),
            shape((HALF, D), bf16),
            shape((BLK, D), bf16),
            shape((BLK, D), f32),
            shape((BLK, D), bf16),
            shape((BLK, D), f32),
            shape((8, D), f32),
        ],
        10,
        room=VMEM_ALL,
    )(n_other, n_mine, g_other, g_mine, packed, packed, fc_bias)


def feed_grad_body(*refs):
    left, (hp_ref, hq_ref, ap_ref, aq_ref, fc_ref, proj_ref) = refs[:8], refs[8:]
    for parts, p_ref, q_ref, o_ref in (
        (left[4:], ap_ref, aq_ref, proj_ref),
        (left[:4], hp_ref, hq_ref, fc_ref),
    ):
        r, p, s, q = parts
        o_ref[...] = (
            mm_tn(r[...], p_ref[:BLK, :])
            + mm_tn(p[...], p_ref[BLK:, :])
            + mm_tn(s[...], q_ref[:BLK, :])
            + mm_tn(q[...], q_ref[BLK:, :])
        ).astype(bf16)


def feed_grad(normed, cots, d_hidden, active):
    part = pl.BlockSpec((BLK, BLK), lambda i: (0, i))
    return kernel_call(
        feed_grad_body,
        (4,),
        [part] * 8 + [whole((HALF, D))] * 4,
        [rows(D)] * 2,
        [shape((D, D), bf16)] * 2,
        9.5,
        room=VMEM_ALL,
    )(*normed, *cots, *d_hidden, *active)


def mid_grad_body(s_ref, r_ref, mid_ref, g_ref, small_ref, dm_ref, low_ref, sum_ref):
    d_normed = s_ref[...] + r_ref[...].astype(f32)
    xhat, root = normalized(mid_ref[...])
    g = g_ref[...].astype(f32)
    d_middle = g + norm_pull(d_normed, xhat, root, small_ref[3:4, :])
    dm_ref[...] = d_middle
    low = d_middle.astype(bf16)
    low_ref[...] = low

    @pl.when(pl.program_id(0) == 0)
    def _():
        sum_ref[...] = jnp.zeros_like(sum_ref)

    sum_ref[0:1, :] += 0.5 * jnp.sum(d_normed * xhat, axis=0, keepdims=True)
    sum_ref[1:2, :] += 0.5 * jnp.sum(d_normed, axis=0, keepdims=True)
    sum_ref[2:3, :] += 0.5 * jnp.sum(g, axis=0, keepdims=True)
    sum_ref[3:4, :] += 0.5 * jnp.sum(low.astype(f32), axis=0, keepdims=True)


def mid_grad(s, far, middle, cot, smalls):
    return kernel_call(
        mid_grad_body,
        (2,),
        [THIN] * 4 + [whole((8, D))],
        [THIN] * 2 + [whole((8, D))],
        [shape((BLK, D), f32), shape((BLK, D), bf16), shape((8, D), f32)],
        2,
    )(s, far, middle, cot, smalls)


def context_grad_body(p_ref, q_ref, r_ref, s_ref, w_ref, o_ref):
    for k, ref in enumerate((p_ref, q_ref, r_ref, s_ref)):
        o_ref[k * BLK : (k + 1) * BLK, :] = mm(ref[...], w_ref[...]).astype(bf16)


def context_grad(parts, packed):
    return kernel_call(
        context_grad_body,
        (1,),
        [PART] * 4 + [OUT_COLUMNS],
        whole((SEQ, 256)),
        shape((SEQ, 256), bf16),
        1,
    )(*parts, packed)


def norm_one_part(q_ref, k_ref, v_ref, w_ref):
    return (
        mm_nt(q_ref[...], w_ref[:, :256])
        + mm_nt(k_ref[...], w_ref[:, 256:512])
        + mm_nt(v_ref[...], w_ref[:, 512:768])
    )


def norm_one_other_body(q_ref, k_ref, v_ref, w_ref, o_ref):
    o_ref[...] = norm_one_part(q_ref, k_ref, v_ref, w_ref).astype(bf16)


def norm_one_other(dq, dk, dv, packed):
    return kernel_call(
        norm_one_other_body,
        (2,),
        [rows(256, lambda i: i + 2)] * 3 + [whole((D, 768))],
        rows(D),
        shape((HALF, D), bf16),
        2,
    )(dq, dk, dv, packed)


def norm_one_mine_body(h_ref, q_ref, k_ref, v_ref, w_ref, r_ref, here_ref, there_ref):
    total = norm_one_part(q_ref, k_ref, v_ref, w_ref) + r_ref[...].astype(f32)

    @pl.when(pl.program_id(0) == 0)
    def _():
        there_ref[...] = total.astype(bf16)

    @pl.when(pl.program_id(0) == 1)
    def _():
        here_ref[...] = total


def norm_one_mine(h, dq, dk, dv, packed, received):
    def turned(width):
        return pl.BlockSpec((BLK, width), lambda i, h_ref: (jnp.where(i == 1, h_ref[0], 1 - h_ref[0]), 0))

    return kernel_call(
        norm_one_mine_body,
        (2,),
        [turned(256)] * 3 + [whole((D, 768)), turned(D)],
        [PART] * 2,
        [shape((BLK, D), f32), shape((BLK, D), bf16)],
        3,
        prefetch=1,
    )(h, dq, dk, dv, packed, received)


def attn_grads_body(
    n_ref, q_ref, k_ref, v_ref, mp_ref, mq_ref, mr_ref, ms_ref, c_ref, w_ref, vp_ref, vq_ref, f0_ref, f1_ref, o_ref, sums
):
    step = pl.program_id(0)

    @pl.when(step == 0)
    def _():
        for p, ref in enumerate((q_ref, k_ref, v_ref)):
            sums[0:1, p * 256 : (p + 1) * 256] = jnp.sum(
                ref[...].astype(f32), axis=0, keepdims=True
            )

    n = n_ref[...]
    gain = w_ref[:, 1024:1025].astype(f32)
    offset = w_ref[:, 1025:1026].astype(f32)
    by_gain = jnp.zeros((BLK, 1), f32)
    by_bias = jnp.zeros((BLK, 1), f32)
    for p, ref in enumerate((q_ref, k_ref, v_ref)):
        cut = slice(p * 256, (p + 1) * 256)
        raw = mm_tn(n, ref[...])
        total = sums[0:1, cut]
        weight = w_ref[:, cut].astype(f32)
        by_gain += jnp.sum(weight * raw, axis=1, keepdims=True)
        by_bias += jnp.sum(weight * total, axis=1, keepdims=True)
        o_ref[:, cut] = (raw * gain + offset * total).astype(bf16)
    out = jnp.zeros((BLK, 256), f32)
    for k, ref in enumerate((mp_ref, mq_ref, mr_ref, ms_ref)):
        out += mm_tn(ref[...], c_ref[k * BLK : (k + 1) * BLK, :])
    o_ref[:, 768:1024] = out.astype(bf16)
    row = lax.broadcasted_iota(jnp.int32, (BLK, 1), 0)
    owner, inner = step * (BLK // 32) + row // 32, row % 32
    columns = [by_gain, by_bias] + [
        picked(vp_ref[k : k + 1, :] + vq_ref[k : k + 1, :], row) for k in range(4)
    ]
    columns.append(picked(f0_ref[0:1, :] + f1_ref[0:1, :], inner // 4 * 128 + owner * 4 + inner % 4))
    lane = inner % 8 // 2 * HD + owner * 2 + inner % 2
    from_q = picked(sums[0:1, 0:256], lane)
    from_v = picked(sums[0:1, 512:768], lane)
    columns.append(jnp.where(inner < 8, from_q, from_v))
    o_ref[:, 1024:1152] = side_columns(columns, BLK)


def attn_grads(xhat, dq, dk, dv, d_mids, context, packed, sums_p, sums_q, fc0, fc1):
    return kernel_call(
        attn_grads_body,
        (4,),
        [pl.BlockSpec((SEQ, BLK), lambda i: (0, i))]
        + [whole((SEQ, 256))] * 3
        + [pl.BlockSpec((BLK, BLK), lambda i: (0, i))] * 4
        + [whole((SEQ, 256)), rows(1152)]
        + [pl.BlockSpec((8, BLK), lambda i: (0, i))] * 2
        + [whole((8, D))] * 2,
        rows(1152),
        shape((D, 1152), bf16),
        6.5,
        scratch=[pltpu.VMEM((8, 768), f32)],
    )(xhat, dq, dk, dv, *d_mids, context, packed, sums_p, sums_q, fc0, fc1)


def input_grad_body(x_ref, a_ref, b_ref, dm_ref, small_ref, o_ref):
    d_normed = a_ref[...] + b_ref[...].astype(f32)
    xhat, root = normalized(x_ref[...].astype(f32))
    o_ref[...] = dm_ref[...] + norm_pull(d_normed, xhat, root, small_ref[0:1, :])


def input_grad_rows(tokens, here, far, d_middle, smalls):
    return kernel_call(
        input_grad_body,
        (2,),
        [THIN] * 4 + [whole((8, D))],
        THIN,
        shape((BLK, D), f32),
        1.5,
    )(tokens, here, far, d_middle, smalls)


def swap(values, axis):
    return lax.ppermute(values, axis, SWAP)


def sent_to_owners(grad):
    return lax.all_to_all(grad.reshape(16, 64, grad.shape[1]), XZ, 0, 0, tiled=True)


def summed_along_z(values):
    z = lax.axis_index("z")
    blocks = values.reshape(4, 64, values.shape[1])

    def block(k):
        return lax.dynamic_index_in_dim(blocks, (z + k) % 4, 0, keepdims=False)

    total = block(0).astype(f32)
    for k in (1, 2, 3):
        turn = [(j, (j + k) % 4) for j in range(4)]
        total += lax.ppermute(block(k), "z", turn).astype(f32)
    return total


def owned(total):
    yl = lax.axis_index("yl")
    here = lax.dynamic_slice_in_dim(total, yl * 32, 32, 0)
    there = lax.dynamic_slice_in_dim(total, (1 - yl) * 32, 32, 0)
    return here + swap(there.astype(bf16), "yl").astype(f32)


def shards(
    tokens,
    cotangent,
    segments,
    ln1_gain,
    ln1_bias,
    w_qkv,
    bias_qv,
    w_out,
    bias_out,
    ln2_gain,
    ln2_bias,
    w_fc,
    bias_fc,
    w_proj,
    bias_proj,
):
    yh, core, yl = lax.axis_index("yh"), lax.axis_index("core"), lax.axis_index("yl")
    pack = packed_shards(
        [ln1_gain, ln1_bias, bias_out, ln2_gain, ln2_bias, bias_proj],
        bias_qv,
        bias_fc,
        w_qkv,
        w_out,
        w_fc,
        w_proj,
    )
    pack, tokens_late = lax.optimization_barrier((pack, tokens))
    neighbour = swap(pack, "yl")
    both = jnp.where(
        yl == 0, jnp.concatenate([pack, neighbour]), jnp.concatenate([neighbour, pack])
    )
    at = jnp.arange(4, dtype=jnp.int32)
    loc = at // 2 + 2 * (at % 2 != core).astype(jnp.int32)

    def by_half(own, far):
        return jnp.where(yh == 0, own, far), jnp.where(yh == 0, far, own)

    segr = segments.reshape(1, SEQ).astype(f32)
    packed_attn = lax.all_to_all(
        jnp.broadcast_to(both[:, :1152], (16, 64, 1152)), XZ, 0, 0, tiled=True
    ).reshape(D, 1152)
    x_p, x_q = by_half(tokens, swap(tokens_late, "yh"))
    x_mine = jnp.concatenate([x_p, x_q])
    x_all = jnp.concatenate([x_mine, swap(x_mine, "core")])
    small_t = packed_attn[:, 1024:1032].T
    second, small_t, x_all = lax.optimization_barrier((both[:, 1152:], small_t, x_all))
    packed = lax.all_gather(second, XZ, axis=0, tiled=True)

    smalls = small_t.astype(f32)
    qv = small_t[6].reshape(32, 32)[:, :16].reshape(32, 2, 4, 2).transpose(1, 2, 0, 3)
    qv = qv.reshape(2, 256).astype(f32)
    bias_row = jnp.concatenate([qv[0], jnp.zeros((256,), f32), qv[1]])[None]
    fc_bias = small_t[7].reshape(32, 8, 4).transpose(1, 0, 2).reshape(1, D).astype(f32)

    xhat_one, joined = qkv_rows(x_all, packed_attn, smalls, bias_row)
    joined, cot_late = lax.optimization_barrier((joined, cotangent))
    c_p, c_q = by_half(cotangent, swap(cot_late, "yh"))
    context = attend_forward(loc, segr, joined)
    context, c_p, c_q = lax.optimization_barrier((context, c_p, c_q))
    c_r, c_s = swap(c_p, "core"), swap(c_q, "core")
    received = swap(out_other(context, packed_attn), "core")
    s_p, s_q, low_p, low_q = out_mine(context, packed_attn, received)
    far_p, far_q = swap(low_p, "yh"), swap(low_q, "yh")
    far_p, fc_bias = lax.optimization_barrier((far_p, fc_bias))

    mid_p, n_p = middle_rows(x_p, s_p, far_p, smalls)
    n_r = swap(n_p, "core")
    act_p, dh_p, mo_p, mm_p, do_p, dm_p, sum_p = feed(n_r, n_p, c_r, c_p, packed, fc_bias)
    do_p, far_q = lax.optimization_barrier((do_p, far_q))
    mid_q, n_q = middle_rows(x_q, s_q, far_q, smalls)
    n_s = swap(n_q, "core")
    dn_p = dm_p + swap(do_p, "core").astype(f32)
    dn_p_low, n_q = lax.optimization_barrier((dn_p.astype(bf16), n_q))
    r_p = swap(dn_p_low, "yh")
    act_q, dh_q, mo_q, mm_q, do_q, dm_q, sum_q = feed(n_s, n_q, c_s, c_q, packed, fc_bias)
    mo_q, r_p = lax.optimization_barrier((mo_q, r_p))
    dn_q = dm_q + swap(do_q, "core").astype(f32)
    dn_q_low, dh_q, act_q = lax.optimization_barrier((dn_q.astype(bf16), dh_q, act_q))
    r_q = swap(dn_q_low, "yh")
    grads_fc, grads_proj = feed_grad(
        (n_r, n_p, n_s, n_q), (c_r, c_p, c_s, c_q), (dh_p, dh_q), (act_p, act_q)
    )
    dmid_p, dl_p, vec_p = mid_grad(dn_p, r_p, mid_p, c_p, smalls)
    dl_p, r_q = lax.optimization_barrier((dl_p, r_q))
    dl_r = swap(dl_p, "core")
    grads_fc, r_q = lax.optimization_barrier((grads_fc, r_q))
    fc_share = lax.psum_scatter(grads_fc, "x", scatter_dimension=0, tiled=True)
    fc_share = summed_along_z(fc_share)
    proj_parts = sent_to_owners(grads_proj)
    dmid_q, dl_q, vec_q = mid_grad(dn_q, r_q, mid_q, c_q, smalls)
    dl_s = swap(dl_q, "core")
    d_mids = (dl_p, dl_q, dl_r, dl_s)
    d_context = context_grad(d_mids, packed_attn)

    dmid_own, _ = by_half(dmid_p, dmid_q)

    dq, dk, dv = attend_backward(loc, segr, joined, d_context)
    grads = attn_grads(
        xhat_one, dq, dk, dv, d_mids, context, packed_attn, vec_p, vec_q, sum_p, sum_q
    )
    grads, dq, dk, dv = lax.optimization_barrier((grads, dq, dk, dv))
    grads, proj_parts = lax.optimization_barrier((grads, proj_parts))
    parts = sent_to_owners(grads)
    grad_proj = owned(jnp.sum(proj_parts.astype(f32), axis=0))
    from_core = swap(norm_one_other(dq, dk, dv, packed_attn), "core")
    d_here, d_there = norm_one_mine(
        yh.astype(jnp.int32).reshape(1), dq, dk, dv, packed_attn, from_core
    )
    far_one = swap(d_there, "yh")
    mo_p, mo_q, d_here = lax.optimization_barrier((mo_p, mo_q, d_here))
    mlp_p = mm_p + swap(mo_p, "core").astype(f32)
    mlp_q = mm_q + swap(mo_q, "core").astype(f32)
    mlp_own, mlp_far = by_half(mlp_p, mlp_q)
    mid_own, _ = by_half(mid_p, mid_q)
    r_mlp = swap(mlp_far.astype(bf16), "yh")
    input_grad = input_grad_rows(tokens, d_here, far_one, dmid_own, smalls)
    parts, fc_share, grad_proj = lax.optimization_barrier((parts, fc_share, grad_proj))
    grad_fc = owned(fc_share)
    grad_attn = owned(jnp.sum(parts.astype(f32), axis=0))
    grad_qkv, grad_out = grad_attn[:, :768].reshape(32, 3, 256), grad_attn[:, 768:1024].T
    small = grad_attn[:, 1024:1032]
    small, r_mlp = lax.optimization_barrier((small, r_mlp))
    mixed = (mid_own + (mlp_own + r_mlp.astype(f32)) + smalls[5:6]).astype(bf16)
    turned = [
        lax.ppermute(small, TP, [(k, (k + turn) % 4) for k in range(4)]) for turn in (1, 2, 3)
    ]
    t = (2 * yh + core).astype(jnp.int32).reshape(1)
    outs = small_out(t, small, turned)
    return (
        mixed,
        input_grad,
        outs[0].reshape(8),
        outs[1].reshape(8),
        grad_qkv,
        outs[7].transpose(0, 2, 1),
        grad_out,
        outs[5].reshape(32),
        outs[2].reshape(8),
        outs[3].reshape(8),
        grad_fc,
        outs[6].T,
        grad_proj.T,
        outs[4].reshape(32),
    )


def solution(mesh):
    fine = Mesh(mesh.devices.reshape(4, 4, 2, 2, 2), ALL)
    tok, dp, tp = P(ALL, None), DP, TP
    return jax.shard_map(
        shards,
        mesh=fine,
        in_specs=(
            tok,
            tok,
            P(dp),
            P(dp),
            P(dp),
            P(dp, None, tp),
            P(None, tp, dp),
            P(tp, dp),
            P(dp),
            P(dp),
            P(dp),
            P(dp, tp),
            P(tp, dp),
            P(tp, dp),
            P(dp),
        ),
        out_specs=(
            tok,
            tok,
            P(ALL),
            P(ALL),
            P(dp, None, tp),
            P(None, tp, dp),
            P(tp, dp),
            P(dp),
            P(ALL),
            P(ALL),
            P(dp, tp),
            P(tp, dp),
            P(tp, dp),
            P(dp),
        ),
        check_vma=False,
    )
```

```python
import functools

import jax
import jax.numpy as jnp
from jax import lax
from jax.experimental import pallas as pl
from jax.experimental.pallas import tpu as pltpu
from jax.sharding import Mesh
from jax.sharding import PartitionSpec as P

HD = 64
SEQ = 1024
D = 1024
BLK = 256
HALF = 512
EPS = 1e-05
GELU_C = 0.7978845608028654
GELU_A = 0.044715
DP = ("x", "z", "yl")
TP = ("yh", "core")
XZ = ("x", "z")
ALL = DP + TP
SWAP = [(0, 1), (1, 0)]
f32 = jnp.float32
bf16 = jnp.bfloat16
VMEM_BYTES = 32 * 1024 * 1024
VMEM_ALL = 62 * 1024 * 1024


def kernel_call(
    body, grid, in_specs, out_specs, out_shape, busy_us, prefetch=0, scratch=(), room=VMEM_BYTES
):
    return pl.pallas_call(
        body,
        out_shape=out_shape,
        grid_spec=pltpu.PrefetchScalarGridSpec(
            num_scalar_prefetch=prefetch,
            grid=grid,
            in_specs=in_specs,
            out_specs=out_specs,
            scratch_shapes=scratch,
        ),
        compiler_params=pltpu.CompilerParams(vmem_limit_bytes=room),
        cost_estimate=pl.CostEstimate(
            flops=int(busy_us * 1.15e9), bytes_accessed=int(busy_us * 3e6), transcendentals=0
        ),
    )


def shape(dims, dtype):
    return jax.ShapeDtypeStruct(dims, dtype)


def mm(a, b):
    return jnp.dot(a, b, preferred_element_type=f32)


def mm_nt(a, b):
    return lax.dot_general(a, b, (((1,), (1,)), ((), ())), preferred_element_type=f32)


def mm_tn(a, b):
    return lax.dot_general(a, b, (((0,), (0,)), ((), ())), preferred_element_type=f32)


def normalized(values):
    centered = values - jnp.mean(values, axis=-1, keepdims=True)
    variance = jnp.mean(centered * centered, axis=-1, keepdims=True)
    root = lax.rsqrt(variance + EPS)
    return centered * root, root


def norm_pull(grad, xhat, root, gain):
    scaled = grad * gain
    return root * (
        scaled
        - jnp.mean(scaled, axis=-1, keepdims=True)
        - xhat * jnp.mean(scaled * xhat, axis=-1, keepdims=True)
    )


def rows(width, move=lambda i: i, height=BLK):
    return pl.BlockSpec((height, width), lambda i, *_: (move(i), 0))


def whole(dims):
    return pl.BlockSpec(dims, lambda *_: (0,) * len(dims))


def picked(vector, lane):
    at = lax.broadcasted_iota(jnp.int32, (lane.shape[0], vector.shape[1]), 1)
    return jnp.sum(jnp.where(at == lane, vector.astype(f32), 0.0), axis=1, keepdims=True)


def side_columns(columns, height):
    at = lax.broadcasted_iota(jnp.int32, (height, 128), 1)
    small = jnp.zeros((height, 128), f32)
    for k, column in enumerate(columns):
        small = jnp.where(at == k, column, small)
    return small.astype(bf16)


def pack_body(*refs):
    vectors, (qv_ref, fc_ref, qkv_ref, out_ref, w_fc_ref, proj_ref, o_ref) = refs[:6], refs[6:]
    row = lax.broadcasted_iota(jnp.int32, (32, 1), 0)
    columns = [picked(ref[...], row) for ref in vectors]
    inner = row % 2
    qv = jnp.zeros((32, 1), f32)
    for s in range(2):
        for e in range(2):
            found = picked(qv_ref[s, e : e + 1, :], row % 8 // 2)
            qv = jnp.where((row // 8 == s) & (inner == e), found, qv)
    fc = jnp.zeros((32, 1), f32)
    for c in range(4):
        fc = jnp.where(row % 4 == c, picked(fc_ref[c : c + 1, :], row // 4), fc)
    for p in range(3):
        o_ref[:, p * 256 : (p + 1) * 256] = qkv_ref[p]
    o_ref[:, 768:1024] = out_ref[...]
    o_ref[:, 1024:1152] = side_columns(columns + [qv, fc], 32)
    o_ref[:, 1152:2176] = w_fc_ref[...]
    o_ref[:, 2176:3200] = proj_ref[...]


def packed_shards(vectors, bias_qv, bias_fc, w_qkv, w_out, w_fc, w_proj):
    arrays = [v.reshape(1, 32) for v in vectors] + [
        bias_qv.transpose(0, 2, 1),
        bias_fc.T,
        w_qkv.transpose(1, 0, 2),
        w_out.T,
        w_fc,
        w_proj.T,
    ]
    return kernel_call(
        pack_body,
        (1,),
        [whole(a.shape) for a in arrays],
        whole((32, 3200)),
        shape((32, 3200), bf16),
        2,
        room=VMEM_ALL,
    )(*arrays)


def small_out_body(t_ref, small_ref, a_ref, b_ref, c_ref, *outs):
    small = small_ref[...]
    total = small + a_ref[...] + (b_ref[...] + c_ref[...])

    def across(values, column, width, row_of):
        lane = lax.broadcasted_iota(jnp.int32, (32, width), 1)
        row = lax.broadcasted_iota(jnp.int32, (32, width), 0)
        found = jnp.where(row == row_of(lane), values[:, column : column + 1], 0.0)
        return jnp.sum(found, axis=0, keepdims=True)

    for k in range(4):
        outs[k][...] = across(total, k, 8, lambda lane: 8 * t_ref[0] + lane)
    for k in range(2):
        outs[4 + k][...] = across(total, 4 + k, 32, lambda lane: lane)
    for c in range(4):
        outs[6][c : c + 1, :] = across(small, 6, 8, lambda lane, c=c: 4 * lane + c)
    for s in range(2):
        for e in range(2):
            outs[7][s, e : e + 1, :] = across(
                small, 7, 4, lambda lane, s=s, e=e: 8 * s + 2 * lane + e
            )


def small_out(t, small, turned):
    dims = [(1, 8)] * 4 + [(1, 32)] * 2 + [(4, 8), (2, 2, 4)]
    return kernel_call(
        small_out_body,
        (1,),
        [whole((32, 8))] * 4,
        [whole(d) for d in dims],
        [shape(d, f32) for d in dims],
        1,
        prefetch=1,
        room=VMEM_ALL,
    )(t, small, *turned)


def qkv_body(x_ref, w_ref, small_ref, bias_ref, n_ref, j_ref):
    xhat, _ = normalized(x_ref[...].astype(f32))
    low = (xhat * small_ref[0:1, :] + small_ref[1:2, :]).astype(bf16)
    n_ref[...] = xhat.astype(bf16)
    j_ref[...] = (mm(low, w_ref[...]) + bias_ref[...]).astype(bf16)


def qkv_rows(x_all, packed, smalls, bias_row):
    return kernel_call(
        qkv_body,
        (4,),
        [rows(D), whole((D, 768)), whole((8, D)), whole((1, 768))],
        [rows(D), rows(768)],
        [shape((SEQ, D), bf16), shape((SEQ, 768), bf16)],
        4,
    )(x_all, packed, smalls, bias_row)


def allowed_block(segr_ref, s):
    width = (s + 1) * BLK
    row = lax.broadcasted_iota(jnp.int32, (BLK, 1), 0)
    same = picked(segr_ref[:, s * BLK : width], row) == segr_ref[:, :width]
    row_at = lax.broadcasted_iota(jnp.int32, (BLK, width), 0) + s * BLK
    key_at = lax.broadcasted_iota(jnp.int32, (BLK, width), 1)
    return same & (key_at <= row_at)


def place(loc_ref, s):
    return pl.ds(pl.multiple_of(loc_ref[s] * BLK, BLK), BLK)


def softmax_rows(scores, mask):
    scores = jnp.where(mask, scores, -1e30)
    highest = jnp.max(scores, axis=-1, keepdims=True)
    expanded = jnp.exp(scores - highest)
    return expanded * (1.0 / jnp.sum(expanded, axis=-1, keepdims=True))


def attend_body(loc_ref, segr_ref, q_ref, k_ref, v_ref, o_ref, kn, vn):
    first = lax.broadcasted_iota(jnp.int32, (1, 128), 1) < HD
    for s in range(4):
        kn[s * BLK : (s + 1) * BLK, :] = k_ref[place(loc_ref, s), :]
        vn[s * BLK : (s + 1) * BLK, :] = v_ref[place(loc_ref, s), :]
    for s in range(4):
        width = (s + 1) * BLK
        mask = allowed_block(segr_ref, s)
        q = q_ref[place(loc_ref, s), :] * jnp.asarray(HD**-0.5, bf16)
        done = []
        for mine in (first, ~first):
            qh = jnp.where(mine, q, jnp.zeros_like(q))
            probs = softmax_rows(mm_nt(qh, kn[:width, :]), mask).astype(bf16)
            done.append(mm(probs, vn[:width, :]))
        o_ref[place(loc_ref, s), :] = jnp.where(first, done[0], done[1]).astype(bf16)


def column_block(at):
    return pl.BlockSpec((SEQ, 128), lambda p, *_: (0, at + p))


def attend_forward(loc, segr, joined):
    return kernel_call(
        attend_body,
        (2,),
        [whole((1, SEQ)), column_block(0), column_block(2), column_block(4)],
        column_block(0),
        shape((SEQ, 256), bf16),
        9.5,
        prefetch=1,
        scratch=[pltpu.VMEM((SEQ, 128), bf16)] * 2,
    )(loc, segr, joined, joined, joined)


def attend_back_body(
    loc_ref, segr_ref, q_ref, k_ref, v_ref, d_ref, dq_ref, dk_ref, dv_ref, kn, vn, dk, dv
):
    first = lax.broadcasted_iota(jnp.int32, (1, 128), 1) < HD
    for s in range(4):
        kn[s * BLK : (s + 1) * BLK, :] = k_ref[place(loc_ref, s), :]
        vn[s * BLK : (s + 1) * BLK, :] = v_ref[place(loc_ref, s), :]
    for s in (3, 2, 1, 0):
        width = (s + 1) * BLK
        mask = allowed_block(segr_ref, s)
        q = q_ref[place(loc_ref, s), :] * jnp.asarray(HD**-0.5, bf16)
        d = d_ref[place(loc_ref, s), :]
        keys = kn[:width, :]
        values = vn[:width, :]
        dq_sum, dk_sum, dv_sum = [], [], []
        for mine in (first, ~first):
            qh = jnp.where(mine, q, jnp.zeros_like(q))
            dh = jnp.where(mine, d, jnp.zeros_like(d))
            probs = softmax_rows(mm_nt(qh, keys), mask)
            d_probs = mm_nt(dh, values)
            d_scores = (
                probs * (d_probs - jnp.sum(probs * d_probs, axis=-1, keepdims=True))
            ).astype(bf16)
            dq_sum.append(mm(d_scores, keys))
            dk_sum.append(mm_tn(d_scores, qh))
            dv_sum.append(mm_tn(probs.astype(bf16), dh))
        dq = jnp.where(first, dq_sum[0], dq_sum[1]) * (HD**-0.5)
        dq_ref[place(loc_ref, s), :] = dq.astype(bf16)
        if s == 3:
            dk[...] = dk_sum[0] + dk_sum[1]
            dv[...] = dv_sum[0] + dv_sum[1]
        else:
            dk[:width, :] += dk_sum[0] + dk_sum[1]
            dv[:width, :] += dv_sum[0] + dv_sum[1]
    for s in range(4):
        dk_ref[place(loc_ref, s), :] = dk[s * BLK : (s + 1) * BLK, :].astype(bf16)
        dv_ref[place(loc_ref, s), :] = dv[s * BLK : (s + 1) * BLK, :].astype(bf16)


def attend_backward(loc, segr, joined, d_context):
    return kernel_call(
        attend_back_body,
        (2,),
        [
            whole((1, SEQ)),
            column_block(0),
            column_block(2),
            column_block(4),
            column_block(0),
        ],
        [column_block(0)] * 3,
        [shape((SEQ, 256), bf16)] * 3,
        14,
        prefetch=1,
        scratch=[pltpu.VMEM((SEQ, 128), bf16)] * 2 + [pltpu.VMEM((SEQ, 128), f32)] * 2,
    )(loc, segr, joined, joined, joined, d_context)


def out_other_body(c_ref, w_ref, o_ref):
    o_ref[...] = mm_nt(c_ref[...], w_ref[...]).astype(bf16)


PART = whole((BLK, D))
THIN = rows(D, height=128)
OUT_COLUMNS = pl.BlockSpec((D, 256), lambda *_: (0, 3))
FC_COLUMNS = pl.BlockSpec((D, D), lambda *_: (0, 0))
PROJ_COLUMNS = pl.BlockSpec((D, D), lambda *_: (0, 1))


def out_other(context, packed):
    return kernel_call(
        out_other_body,
        (2,),
        [rows(256, lambda i: i + 2), OUT_COLUMNS],
        rows(D),
        shape((HALF, D), bf16),
        1.5,
    )(context, packed)


def out_mine_body(c_ref, w_ref, r_ref, p_ref, q_ref, p_low_ref, q_low_ref):
    total = mm_nt(c_ref[...], w_ref[...]) + r_ref[...].astype(f32)

    @pl.when(pl.program_id(0) == 0)
    def _():
        p_ref[...] = total
        p_low_ref[...] = total.astype(bf16)

    @pl.when(pl.program_id(0) == 1)
    def _():
        q_ref[...] = total
        q_low_ref[...] = total.astype(bf16)


def out_mine(context, packed, received):
    return kernel_call(
        out_mine_body,
        (2,),
        [rows(256), OUT_COLUMNS, rows(D)],
        [PART] * 4,
        [shape((BLK, D), f32)] * 2 + [shape((BLK, D), bf16)] * 2,
        2,
        room=VMEM_ALL,
    )(context, packed, received)


def middle_body(x_ref, s_ref, r_ref, small_ref, mid_ref, n_ref):
    total = s_ref[...] + r_ref[...].astype(f32)
    middle = x_ref[...].astype(f32) + total + small_ref[2:3, :]
    mid_ref[...] = middle
    xhat, _ = normalized(middle)
    n_ref[...] = (xhat * small_ref[3:4, :] + small_ref[4:5, :]).astype(bf16)


def middle_rows(x, s, far, smalls):
    return kernel_call(
        middle_body,
        (2,),
        [THIN] * 3 + [whole((8, D))],
        [THIN] * 2,
        [shape((BLK, D), f32), shape((BLK, D), bf16)],
        1,
        room=VMEM_ALL,
    )(x, s, far, smalls)


def feed_body(
    no_ref,
    nm_ref,
    go_ref,
    gm_ref,
    fc_ref,
    proj_ref,
    b_ref,
    a_ref,
    dh_ref,
    mo_ref,
    mm_ref,
    do_ref,
    dm_ref,
    sum_ref,
):
    other = pl.program_id(0) == 0
    n = jnp.where(other, no_ref[...], nm_ref[...])
    g = jnp.where(other, go_ref[...], gm_ref[...])

    @pl.when(other)
    def _():
        sum_ref[...] = jnp.zeros_like(sum_ref)

    for at in range(0, D, BLK):
        cut = slice(at, at + BLK)
        hidden = mm(n, fc_ref[:, cut]) + b_ref[:, cut]
        d_active = mm(g, proj_ref[:, cut])
        squared = hidden * hidden
        bent = jnp.tanh(hidden * (GELU_C + (GELU_A * GELU_C) * squared))
        half = 0.5 + 0.5 * bent
        slope = half + (0.5 * hidden) * (1.0 - bent * bent) * (
            GELU_C + (3.0 * GELU_A * GELU_C) * squared
        )
        d_hidden = (d_active * slope).astype(bf16)
        a_ref[:, cut] = (hidden * half).astype(bf16)
        dh_ref[:, cut] = d_hidden
        sum_ref[0:1, cut] += jnp.sum(d_hidden.astype(f32), axis=0, keepdims=True)
    d_normed = mm_nt(dh_ref[...], fc_ref[...])
    mixed = mm_nt(a_ref[...], proj_ref[...])

    @pl.when(other)
    def _():
        do_ref[...] = d_normed.astype(bf16)
        mo_ref[...] = mixed.astype(bf16)

    @pl.when(jnp.logical_not(other))
    def _():
        dm_ref[...] = d_normed
        mm_ref[...] = mixed


def feed(n_other, n_mine, g_other, g_mine, packed, fc_bias):
    return kernel_call(
        feed_body,
        (2,),
        [PART] * 4 + [FC_COLUMNS, PROJ_COLUMNS, whole((1, D))],
        [rows(D)] * 2 + [PART] * 4 + [whole((8, D))],
        [
            shape((HALF, D), bf16),
            shape((HALF, D), bf16),
            shape((BLK, D), bf16),
            shape((BLK, D), f32),
            shape((BLK, D), bf16),
            shape((BLK, D), f32),
            shape((8, D), f32),
        ],
        10,
        room=VMEM_ALL,
    )(n_other, n_mine, g_other, g_mine, packed, packed, fc_bias)


def feed_grad_body(*refs):
    left, (hp_ref, hq_ref, ap_ref, aq_ref, fc_ref, proj_ref) = refs[:8], refs[8:]
    for parts, p_ref, q_ref, o_ref in (
        (left[4:], ap_ref, aq_ref, proj_ref),
        (left[:4], hp_ref, hq_ref, fc_ref),
    ):
        r, p, s, q = parts
        o_ref[...] = (
            mm_tn(r[...], p_ref[:BLK, :])
            + mm_tn(p[...], p_ref[BLK:, :])
            + mm_tn(s[...], q_ref[:BLK, :])
            + mm_tn(q[...], q_ref[BLK:, :])
        ).astype(bf16)


def feed_grad(normed, cots, d_hidden, active):
    part = pl.BlockSpec((BLK, BLK), lambda i: (0, i))
    return kernel_call(
        feed_grad_body,
        (4,),
        [part] * 8 + [whole((HALF, D))] * 4,
        [rows(D)] * 2,
        [shape((D, D), bf16)] * 2,
        9.5,
        room=VMEM_ALL,
    )(*normed, *cots, *d_hidden, *active)


def mid_grad_body(s_ref, r_ref, mid_ref, g_ref, small_ref, dm_ref, low_ref, sum_ref):
    d_normed = s_ref[...] + r_ref[...].astype(f32)
    xhat, root = normalized(mid_ref[...])
    g = g_ref[...].astype(f32)
    d_middle = g + norm_pull(d_normed, xhat, root, small_ref[3:4, :])
    dm_ref[...] = d_middle
    low = d_middle.astype(bf16)
    low_ref[...] = low

    @pl.when(pl.program_id(0) == 0)
    def _():
        sum_ref[...] = jnp.zeros_like(sum_ref)

    sum_ref[0:1, :] += 0.5 * jnp.sum(d_normed * xhat, axis=0, keepdims=True)
    sum_ref[1:2, :] += 0.5 * jnp.sum(d_normed, axis=0, keepdims=True)
    sum_ref[2:3, :] += 0.5 * jnp.sum(g, axis=0, keepdims=True)
    sum_ref[3:4, :] += 0.5 * jnp.sum(low.astype(f32), axis=0, keepdims=True)


def mid_grad(s, far, middle, cot, smalls):
    return kernel_call(
        mid_grad_body,
        (2,),
        [THIN] * 4 + [whole((8, D))],
        [THIN] * 2 + [whole((8, D))],
        [shape((BLK, D), f32), shape((BLK, D), bf16), shape((8, D), f32)],
        2,
        room=VMEM_ALL,
    )(s, far, middle, cot, smalls)


def context_grad_body(p_ref, q_ref, r_ref, s_ref, w_ref, o_ref):
    for k, ref in enumerate((p_ref, q_ref, r_ref, s_ref)):
        o_ref[k * BLK : (k + 1) * BLK, :] = mm(ref[...], w_ref[...]).astype(bf16)


def context_grad(parts, packed):
    return kernel_call(
        context_grad_body,
        (1,),
        [PART] * 4 + [OUT_COLUMNS],
        whole((SEQ, 256)),
        shape((SEQ, 256), bf16),
        1,
    )(*parts, packed)


def norm_one_part(q_ref, k_ref, v_ref, w_ref):
    return (
        mm_nt(q_ref[...], w_ref[:, :256])
        + mm_nt(k_ref[...], w_ref[:, 256:512])
        + mm_nt(v_ref[...], w_ref[:, 512:768])
    )


def norm_one_other_body(q_ref, k_ref, v_ref, w_ref, o_ref):
    o_ref[...] = norm_one_part(q_ref, k_ref, v_ref, w_ref).astype(bf16)


def norm_one_other(dq, dk, dv, packed):
    return kernel_call(
        norm_one_other_body,
        (2,),
        [rows(256, lambda i: i + 2)] * 3 + [whole((D, 768))],
        rows(D),
        shape((HALF, D), bf16),
        2,
    )(dq, dk, dv, packed)


def norm_one_mine_body(h_ref, q_ref, k_ref, v_ref, w_ref, r_ref, here_ref, there_ref):
    total = norm_one_part(q_ref, k_ref, v_ref, w_ref) + r_ref[...].astype(f32)

    @pl.when(pl.program_id(0) == 0)
    def _():
        there_ref[...] = total.astype(bf16)

    @pl.when(pl.program_id(0) == 1)
    def _():
        here_ref[...] = total


def norm_one_mine(h, dq, dk, dv, packed, received):
    def turned(width):
        return pl.BlockSpec((BLK, width), lambda i, h_ref: (jnp.where(i == 1, h_ref[0], 1 - h_ref[0]), 0))

    return kernel_call(
        norm_one_mine_body,
        (2,),
        [turned(256)] * 3 + [whole((D, 768)), turned(D)],
        [PART] * 2,
        [shape((BLK, D), f32), shape((BLK, D), bf16)],
        3,
        prefetch=1,
    )(h, dq, dk, dv, packed, received)


def attn_grads_body(
    n_ref, q_ref, k_ref, v_ref, mp_ref, mq_ref, mr_ref, ms_ref, c_ref, w_ref, vp_ref, vq_ref, f0_ref, f1_ref, o_ref, sums
):
    step = pl.program_id(0)

    @pl.when(step == 0)
    def _():
        for p, ref in enumerate((q_ref, k_ref, v_ref)):
            sums[0:1, p * 256 : (p + 1) * 256] = jnp.sum(
                ref[...].astype(f32), axis=0, keepdims=True
            )

    n = n_ref[...]
    gain = w_ref[:, 1024:1025].astype(f32)
    offset = w_ref[:, 1025:1026].astype(f32)
    by_gain = jnp.zeros((BLK, 1), f32)
    by_bias = jnp.zeros((BLK, 1), f32)
    for p, ref in enumerate((q_ref, k_ref, v_ref)):
        cut = slice(p * 256, (p + 1) * 256)
        raw = mm_tn(n, ref[...])
        total = sums[0:1, cut]
        weight = w_ref[:, cut].astype(f32)
        by_gain += jnp.sum(weight * raw, axis=1, keepdims=True)
        by_bias += jnp.sum(weight * total, axis=1, keepdims=True)
        o_ref[:, cut] = (raw * gain + offset * total).astype(bf16)
    out = jnp.zeros((BLK, 256), f32)
    for k, ref in enumerate((mp_ref, mq_ref, mr_ref, ms_ref)):
        out += mm_tn(ref[...], c_ref[k * BLK : (k + 1) * BLK, :])
    o_ref[:, 768:1024] = out.astype(bf16)
    row = lax.broadcasted_iota(jnp.int32, (BLK, 1), 0)
    owner, inner = step * (BLK // 32) + row // 32, row % 32
    columns = [by_gain, by_bias] + [
        picked(vp_ref[k : k + 1, :] + vq_ref[k : k + 1, :], row) for k in range(4)
    ]
    columns.append(picked(f0_ref[0:1, :] + f1_ref[0:1, :], inner // 4 * 128 + owner * 4 + inner % 4))
    lane = inner % 8 // 2 * HD + owner * 2 + inner % 2
    from_q = picked(sums[0:1, 0:256], lane)
    from_v = picked(sums[0:1, 512:768], lane)
    columns.append(jnp.where(inner < 8, from_q, from_v))
    o_ref[:, 1024:1152] = side_columns(columns, BLK)


def attn_grads(xhat, dq, dk, dv, d_mids, context, packed, sums_p, sums_q, fc0, fc1):
    return kernel_call(
        attn_grads_body,
        (4,),
        [pl.BlockSpec((SEQ, BLK), lambda i: (0, i))]
        + [whole((SEQ, 256))] * 3
        + [pl.BlockSpec((BLK, BLK), lambda i: (0, i))] * 4
        + [whole((SEQ, 256)), rows(1152)]
        + [pl.BlockSpec((8, BLK), lambda i: (0, i))] * 2
        + [whole((8, D))] * 2,
        rows(1152),
        shape((D, 1152), bf16),
        6.5,
        scratch=[pltpu.VMEM((8, 768), f32)],
    )(xhat, dq, dk, dv, *d_mids, context, packed, sums_p, sums_q, fc0, fc1)


def input_grad_body(x_ref, a_ref, b_ref, dm_ref, small_ref, o_ref):
    d_normed = a_ref[...] + b_ref[...].astype(f32)
    xhat, root = normalized(x_ref[...].astype(f32))
    o_ref[...] = dm_ref[...] + norm_pull(d_normed, xhat, root, small_ref[0:1, :])


def input_grad_rows(tokens, here, far, d_middle, smalls):
    return kernel_call(
        input_grad_body,
        (2,),
        [THIN] * 4 + [whole((8, D))],
        THIN,
        shape((BLK, D), f32),
        1.5,
    )(tokens, here, far, d_middle, smalls)


def swap(values, axis):
    return lax.ppermute(values, axis, SWAP)


def sent_to_owners(grad):
    return lax.all_to_all(grad.reshape(16, 64, grad.shape[1]), XZ, 0, 0, tiled=True)


def summed_along_z(values):
    z = lax.axis_index("z")
    blocks = values.reshape(4, 64, values.shape[1])

    def block(k):
        return lax.dynamic_index_in_dim(blocks, (z + k) % 4, 0, keepdims=False)

    total = block(0).astype(f32)
    for k in (1, 2, 3):
        turn = [(j, (j + k) % 4) for j in range(4)]
        total += lax.ppermute(block(k), "z", turn).astype(f32)
    return total


def owned(total):
    yl = lax.axis_index("yl")
    here = lax.dynamic_slice_in_dim(total, yl * 32, 32, 0)
    there = lax.dynamic_slice_in_dim(total, (1 - yl) * 32, 32, 0)
    return here + swap(there.astype(bf16), "yl").astype(f32)


def shards(
    tokens,
    cotangent,
    segments,
    ln1_gain,
    ln1_bias,
    w_qkv,
    bias_qv,
    w_out,
    bias_out,
    ln2_gain,
    ln2_bias,
    w_fc,
    bias_fc,
    w_proj,
    bias_proj,
):
    yh, core, yl = lax.axis_index("yh"), lax.axis_index("core"), lax.axis_index("yl")
    pack = packed_shards(
        [ln1_gain, ln1_bias, bias_out, ln2_gain, ln2_bias, bias_proj],
        bias_qv,
        bias_fc,
        w_qkv,
        w_out,
        w_fc,
        w_proj,
    )
    pack, tokens_late = lax.optimization_barrier((pack, tokens))
    neighbour = swap(pack, "yl")
    both = jnp.where(
        yl == 0, jnp.concatenate([pack, neighbour]), jnp.concatenate([neighbour, pack])
    )
    at = jnp.arange(4, dtype=jnp.int32)
    loc = at // 2 + 2 * (at % 2 != core).astype(jnp.int32)

    def by_half(own, far):
        return jnp.where(yh == 0, own, far), jnp.where(yh == 0, far, own)

    segr = segments.reshape(1, SEQ).astype(f32)
    packed_attn = lax.all_to_all(
        jnp.broadcast_to(both[:, :1152], (16, 64, 1152)), XZ, 0, 0, tiled=True
    ).reshape(D, 1152)
    x_p, x_q = by_half(tokens, swap(tokens_late, "yh"))
    x_mine = jnp.concatenate([x_p, x_q])
    x_all = jnp.concatenate([x_mine, swap(x_mine, "core")])
    small_t = packed_attn[:, 1024:1032].T
    second, small_t, x_all = lax.optimization_barrier((both[:, 1152:], small_t, x_all))
    packed = lax.all_gather(second, XZ, axis=0, tiled=True)

    smalls = small_t.astype(f32)
    qv = small_t[6].reshape(32, 32)[:, :16].reshape(32, 2, 4, 2).transpose(1, 2, 0, 3)
    qv = qv.reshape(2, 256).astype(f32)
    bias_row = jnp.concatenate([qv[0], jnp.zeros((256,), f32), qv[1]])[None]
    fc_bias = small_t[7].reshape(32, 8, 4).transpose(1, 0, 2).reshape(1, D).astype(f32)

    xhat_one, joined = qkv_rows(x_all, packed_attn, smalls, bias_row)
    joined, cot_late = lax.optimization_barrier((joined, cotangent))
    c_p, c_q = by_half(cotangent, swap(cot_late, "yh"))
    context = attend_forward(loc, segr, joined)
    context, c_p, c_q = lax.optimization_barrier((context, c_p, c_q))
    c_r, c_s = swap(c_p, "core"), swap(c_q, "core")
    received = swap(out_other(context, packed_attn), "core")
    s_p, s_q, low_p, low_q = out_mine(context, packed_attn, received)
    far_p, far_q = swap(low_p, "yh"), swap(low_q, "yh")
    far_p, fc_bias = lax.optimization_barrier((far_p, fc_bias))

    mid_p, n_p = middle_rows(x_p, s_p, far_p, smalls)
    n_r = swap(n_p, "core")
    act_p, dh_p, mo_p, mm_p, do_p, dm_p, sum_p = feed(n_r, n_p, c_r, c_p, packed, fc_bias)
    do_p, far_q = lax.optimization_barrier((do_p, far_q))
    mid_q, n_q = middle_rows(x_q, s_q, far_q, smalls)
    n_s = swap(n_q, "core")
    dn_p = dm_p + swap(do_p, "core").astype(f32)
    dn_p_low, n_q = lax.optimization_barrier((dn_p.astype(bf16), n_q))
    r_p = swap(dn_p_low, "yh")
    act_q, dh_q, mo_q, mm_q, do_q, dm_q, sum_q = feed(n_s, n_q, c_s, c_q, packed, fc_bias)
    mo_q, r_p = lax.optimization_barrier((mo_q, r_p))
    dn_q = dm_q + swap(do_q, "core").astype(f32)
    dn_q_low, dh_q, act_q = lax.optimization_barrier((dn_q.astype(bf16), dh_q, act_q))
    r_q = swap(dn_q_low, "yh")
    grads_fc, grads_proj = feed_grad(
        (n_r, n_p, n_s, n_q), (c_r, c_p, c_s, c_q), (dh_p, dh_q), (act_p, act_q)
    )
    dmid_p, dl_p, vec_p = mid_grad(dn_p, r_p, mid_p, c_p, smalls)
    dl_p, r_q = lax.optimization_barrier((dl_p, r_q))
    dl_r = swap(dl_p, "core")
    grads_fc, r_q = lax.optimization_barrier((grads_fc, r_q))
    fc_share = lax.psum_scatter(grads_fc, "x", scatter_dimension=0, tiled=True)
    fc_share = summed_along_z(fc_share)
    proj_parts = sent_to_owners(grads_proj)
    dmid_q, dl_q, vec_q = mid_grad(dn_q, r_q, mid_q, c_q, smalls)
    dl_s = swap(dl_q, "core")
    d_mids = (dl_p, dl_q, dl_r, dl_s)
    d_context = context_grad(d_mids, packed_attn)

    dmid_own, _ = by_half(dmid_p, dmid_q)

    dq, dk, dv = attend_backward(loc, segr, joined, d_context)
    grads = attn_grads(
        xhat_one, dq, dk, dv, d_mids, context, packed_attn, vec_p, vec_q, sum_p, sum_q
    )
    grads, dq, dk, dv = lax.optimization_barrier((grads, dq, dk, dv))
    grads, proj_parts = lax.optimization_barrier((grads, proj_parts))
    parts = sent_to_owners(grads)
    grad_proj = owned(jnp.sum(proj_parts.astype(f32), axis=0))
    from_core = swap(norm_one_other(dq, dk, dv, packed_attn), "core")
    d_here, d_there = norm_one_mine(
        yh.astype(jnp.int32).reshape(1), dq, dk, dv, packed_attn, from_core
    )
    far_one = swap(d_there, "yh")
    mo_p, mo_q, d_here = lax.optimization_barrier((mo_p, mo_q, d_here))
    mlp_p = mm_p + swap(mo_p, "core").astype(f32)
    mlp_q = mm_q + swap(mo_q, "core").astype(f32)
    mlp_own, mlp_far = by_half(mlp_p, mlp_q)
    mid_own, _ = by_half(mid_p, mid_q)
    r_mlp = swap(mlp_far.astype(bf16), "yh")
    input_grad = input_grad_rows(tokens, d_here, far_one, dmid_own, smalls)
    parts, fc_share, grad_proj = lax.optimization_barrier((parts, fc_share, grad_proj))
    grad_fc = owned(fc_share)
    grad_attn = owned(jnp.sum(parts.astype(f32), axis=0))
    grad_qkv, grad_out = grad_attn[:, :768].reshape(32, 3, 256), grad_attn[:, 768:1024].T
    small = grad_attn[:, 1024:1032]
    small, r_mlp = lax.optimization_barrier((small, r_mlp))
    mixed = (mid_own + (mlp_own + r_mlp.astype(f32)) + smalls[5:6]).astype(bf16)
    turned = [
        lax.ppermute(small, TP, [(k, (k + turn) % 4) for k in range(4)]) for turn in (1, 2, 3)
    ]
    t = (2 * yh + core).astype(jnp.int32).reshape(1)
    outs = small_out(t, small, turned)
    return (
        mixed,
        input_grad,
        outs[0].reshape(8),
        outs[1].reshape(8),
        grad_qkv,
        outs[7].transpose(0, 2, 1),
        grad_out,
        outs[5].reshape(32),
        outs[2].reshape(8),
        outs[3].reshape(8),
        grad_fc,
        outs[6].T,
        grad_proj.T,
        outs[4].reshape(32),
    )


def solution(mesh):
    fine = Mesh(mesh.devices.reshape(4, 4, 2, 2, 2), ALL)
    tok, dp, tp = P(ALL, None), DP, TP
    return jax.shard_map(
        shards,
        mesh=fine,
        in_specs=(
            tok,
            tok,
            P(dp),
            P(dp),
            P(dp),
            P(dp, None, tp),
            P(None, tp, dp),
            P(tp, dp),
            P(dp),
            P(dp),
            P(dp),
            P(dp, tp),
            P(tp, dp),
            P(tp, dp),
            P(dp),
        ),
        out_specs=(
            tok,
            tok,
            P(ALL),
            P(ALL),
            P(dp, None, tp),
            P(None, tp, dp),
            P(tp, dp),
            P(dp),
            P(ALL),
            P(ALL),
            P(dp, tp),
            P(tp, dp),
            P(tp, dp),
            P(dp),
        ),
        check_vma=False,
    )
```
